32 devices in a mesh: pipe: 4 (over y, x), dp: 8 (over z, core).
Axes of the slice: x: 2, y: 2, z: 4, core: 2. Of those that a mesh axis runs over, the one named last changes fastest.
Arguments:
- clips: bfloat16 [2, 3, 1024, 1536], P(None, None, 'dp'), may hold values from -6 to 6
- positions: int32 [3, 2, 3, 1024], P(None, None, None, 'dp'), may hold values from 0 to 79, as said below
- out_proj: bfloat16 [4, 1536, 1536], P('pipe', 'dp'), may hold values from -0.15625 to 0.15625
- qk_gains: bfloat16 [4, 2, 128], P('pipe'), may hold values from -1.5 to 1.5
- cotangent: bfloat16 [2, 3, 1024, 1536], P(None, None, 'dp'), may hold values from -0.1875 to 0.1875
Outputs:
- grad_out_proj: float32 [4, 1536, 1536], P('pipe', 'dp')
- grad_gains: float32 [4, 2, 128], P('pipe')
The draws below stay inside these ranges and needn't reach their ends.
Inputs may be any that keep to these rules, and one draw needn't show every extreme that they name: positions[0] is a token's frame, positions[1] its row and positions[2] its column in the latent video.
All inputs are finite; a program needn't handle non-finite values.
Results may differ from the reference program's by a relative error of at most 0.018.
Values may be sent and summed in bfloat16 or wider, within the bound.
No kernel may reach another device: no remote copies, remote signals or barrier semaphores. Data moves between devices by JAX's collectives and lax.ppermute only.
A program may use at most 192 MiB of HBM per device.

```python
import math
import jax
import jax.numpy as jnp
from jax import lax

D = 1536
HEAD = 128
TOK = 128
MICRO = 3
PHASES = 4
TOKENS = 1024


def draw_positions(key, part):
    keys = jax.random.split(key, 3)
    starts = jax.random.randint(keys[0], (2, MICRO, TOKENS // TOK, 1), 0, 30)
    within = jnp.arange(TOK, dtype=jnp.int32)
    frames = (starts + within // 64).reshape(2, MICRO, TOKENS)
    row_ids = jax.random.randint(keys[1], (2, MICRO, TOKENS), 0, 45)
    column_ids = jax.random.randint(keys[2], (2, MICRO, TOKENS), 0, 80)
    row_ids = row_ids.at[:, :, TOKENS - 1].set(0)
    column_ids = column_ids.at[:, :, TOKENS - 1].set(79)
    return jnp.stack([frames, row_ids, column_ids]).astype(jnp.int32)


def levels(stream_key, shape, cuts, low, high):
    factor_of, own = 1.0, jax.random.fold_in(stream_key, 6)
    for position, shards_of in cuts:
        heights = jnp.exp(jax.random.uniform(jax.random.fold_in(own, position), (shards_of,), jnp.float32, low / len(cuts), high / len(cuts)))
        factor_of = factor_of * jnp.repeat(heights, shape[position] // shards_of).reshape([-1 if axis == position else 1 for axis in range(len(shape))])
    return factor_of


def noise(key, dims, scale, reach, cuts=(), kind=jnp.bfloat16):
    level = levels(key, dims, cuts, -0.22, 0.18) if cuts else 1.0
    result = jax.random.normal(key, dims, jnp.float32) * scale * level
    return jnp.minimum(jnp.maximum(result, -reach), reach).astype(kind)


def setup_inputs(seed: int = 0) -> dict:
    arg_keys = jax.random.split(jax.random.key(seed), 6)
    clips = noise(arg_keys[0], (2, MICRO, TOKENS, D), 1.0, 6.0, ((2, 8),))
    positions = draw_positions(jax.random.fold_in(arg_keys[5], 71), 0)
    out_proj = noise(arg_keys[2], (PHASES, D, D), D ** -0.5, 0.15625, ((0, 4), (1, 8)))
    qk_gains = jnp.clip(jax.random.uniform(arg_keys[3], (PHASES, 2, HEAD), jnp.float32, -1.5, 1.5) * levels(arg_keys[3], (PHASES, 2, HEAD), ((0, 4),), -0.4, 0.0), -1.5, 1.5).astype(jnp.bfloat16)
    cotangent = noise(arg_keys[4], (2, MICRO, TOKENS, D), (1.0 / (2 * MICRO * TOKENS) ** 0.5), 0.1875, ((2, 8),))
    return {"clips": clips, "positions": positions, "out_proj": out_proj, "qk_gains": qk_gains, "cotangent": cotangent}


def rotate(values, coords):
    head_size = values.shape[-1]
    first_width = head_size // 8
    rest_width = (head_size - first_width) // 2
    widths = (first_width, rest_width, rest_width)
    pieces = []
    offset = 0
    for axis_index in range(3):
        section = widths[axis_index]
        half_width = section // 2
        segment = values[..., offset:offset + section]
        frequency = 256.0 ** (-2.0 * jnp.arange(half_width, dtype=jnp.float32) / section)
        angles = coords[axis_index].astype(jnp.float32)[:, None] * frequency[None, :]
        cosine = jnp.cos(angles)[:, None, :]
        sine_part = jnp.sin(angles)[:, None, :]
        lower_half = segment[..., :half_width]
        upper_half = segment[..., half_width:]
        pieces.append(lower_half * cosine - upper_half * sine_part)
        pieces.append(lower_half * sine_part + upper_half * cosine)
        offset = offset + section
    return jnp.concatenate(pieces, axis=-1)

def mixing(hidden, gain_pair, coords):
    row_count, channels = hidden.shape
    head_size = gain_pair.shape[-1]
    by_heads = hidden.reshape(row_count, channels // head_size, head_size)
    wide_heads = by_heads.astype(jnp.float32)
    normed = wide_heads * lax.rsqrt(lax.optimization_barrier(jnp.mean(wide_heads * wide_heads, axis=-1, keepdims=True)) + 1e-06)
    queries = rotate(normed * gain_pair[0], coords)
    key_rows = rotate(normed * gain_pair[1], coords)
    scores = jnp.einsum('qhe,khe->hqk', queries, key_rows, precision=lax.Precision.HIGHEST) / math.sqrt(head_size)
    exp_scores = jnp.exp(scores)
    weights = (exp_scores / lax.optimization_barrier(jnp.sum(exp_scores, axis=-1, keepdims=True))).astype(jnp.bfloat16)
    weights_wide = lax.optimization_barrier(weights).astype(jnp.float32)
    mixed_rows = jnp.einsum('hqk,khe->qhe', weights_wide, wide_heads)
    return mixed_rows.reshape(row_count, channels).astype(jnp.bfloat16)

def phase_forward(hidden, gain_pair, coords, weight):
    mixed_rows = mixing(hidden, gain_pair, coords)
    update = jnp.dot(mixed_rows, weight, preferred_element_type=jnp.float32)
    return (hidden.astype(jnp.float32) + update).astype(jnp.bfloat16)

def phase_backward(hidden, gain_pair, coords, weight, grad_out):

    def local_mix(state_rows, gain_values):
        return mixing(state_rows, gain_values, coords)
    mixed_rows, pullback = jax.vjp(local_mix, hidden, gain_pair)
    weight_term = lax.dot_general(mixed_rows, grad_out, (((0,), (0,)), ((), ())), preferred_element_type=jnp.float32)
    grad_mixed = lax.dot_general(grad_out, weight, (((1,), (1,)), ((), ())), preferred_element_type=jnp.float32).astype(jnp.bfloat16)
    grad_hidden, gain_term = pullback(grad_mixed)
    grad_in = (grad_out.astype(jnp.float32) + grad_hidden.astype(jnp.float32)).astype(jnp.bfloat16)
    return (grad_in, weight_term, gain_term)

def reference(clips, positions, out_proj, qk_gains, cotangent):
    phase_count = out_proj.shape[0]
    micro_count = clips.shape[1]
    channels = clips.shape[3]
    group_count = clips.shape[2] // TOK
    batch_count = 2 * micro_count * group_count
    all_rows = clips.reshape(batch_count, TOK, channels)
    coord_rows = jnp.transpose(positions.reshape(3, batch_count, TOK), (1, 0, 2))
    cot_rows = cotangent.reshape(batch_count, TOK, channels)
    gain_table = qk_gains.astype(jnp.float32)
    forward_map = jax.vmap(phase_forward, in_axes=(0, None, 0, None))
    inputs = []
    hidden = all_rows
    for phase_index in range(phase_count):
        inputs.append(hidden)
        hidden = forward_map(hidden, gain_table[phase_index], coord_rows, out_proj[phase_index])
    grad_rows = cot_rows
    weight_grads = [None] * phase_count
    gain_grads = [None] * phase_count
    for phase_index in reversed(range(phase_count)):
        gain_pair = gain_table[phase_index]
        weight = out_proj[phase_index]

        def backward_one(carry, batch_item):
            state_rows, coord_item, grad_item = batch_item
            grad_in, weight_term, gain_term = phase_backward(state_rows, gain_pair, coord_item, weight, grad_item)
            return ((carry[0] + weight_term, carry[1] + gain_term), grad_in)
        start_sums = (jnp.zeros((channels, channels), jnp.float32), jnp.zeros(gain_pair.shape, jnp.float32))
        totals, grad_rows = lax.scan(backward_one, start_sums, (inputs[phase_index], coord_rows, grad_rows))
        weight_grads[phase_index] = totals[0]
        gain_grads[phase_index] = totals[1]
    return (jnp.stack(weight_grads), jnp.stack(gain_grads))
```

```python
import functools
import math

import jax
import jax.numpy as jnp
import numpy as np
from jax import lax
from jax.experimental import pallas as pl
from jax.experimental.pallas import tpu as pltpu
from jax.sharding import PartitionSpec as P

F32 = jnp.float32
BF16 = jnp.bfloat16
VMEM_BYTES = 56 * 1024 * 1024
CORES = 2


def lane_tables(head):
    first = head // 8
    rest = (head - first) // 2
    coord = np.zeros(head, np.int32)
    freq = np.zeros(head, np.float32)
    sign = np.zeros(head, np.float32)
    partner = np.zeros(head, np.int32)
    offset = 0
    for axis, width in enumerate((first, rest, rest)):
        half = width // 2
        for j in range(half):
            low, high = offset + j, offset + j + half
            coord[low] = coord[high] = axis
            freq[low] = freq[high] = 256.0 ** (-2.0 * j / width)
            sign[low], sign[high] = -1.0, 1.0
            partner[low], partner[high] = high, low
        offset += width
    return coord, freq, sign, partner


def swap_lanes(x, partner):
    return jnp.take_along_axis(x, partner, axis=1, mode="promise_in_bounds")


def nt(a, b):
    return lax.dot_general(a, b, (((1,), (1,)), ((), ())), preferred_element_type=F32)


def tn(a, b):
    return lax.dot_general(a, b, (((0,), (0,)), ((), ())), preferred_element_type=F32)


def split(x):
    high = x.astype(BF16)
    return high, (x - high.astype(F32)).astype(BF16)


def fill_tables(tables, cos_ref, sin_ref, gain, first=0):
    for t in range(tables.shape[0]):
        cosine, sine = cos_ref[first + t], sin_ref[first + t]
        tables[t, 0] = cosine * gain[0:1]
        tables[t, 1] = sine * gain[1:2]
        tables[t, 2] = cosine * gain[2:3]
        tables[t, 3] = sine * gain[3:4]


def project(hidden, mixed, weight, out, width):
    def part(i, carry):
        cols = pl.ds(pl.multiple_of(i * width, width), width)
        update = jnp.dot(mixed[...], weight[:, cols], preferred_element_type=F32)
        out[:, cols] = (hidden[:, cols].astype(F32) + update).astype(BF16)
        return carry

    lax.fori_loop(0, out.shape[1] // width, part, 0)


def pull_mixed(grad, weight, grad_mixed, width):
    def part(i, carry):
        cols = pl.ds(pl.multiple_of(i * width, width), width)
        grad_mixed[:, cols] = nt(grad[...], weight[cols, :]).astype(BF16)
        return carry

    lax.fori_loop(0, grad_mixed.shape[1] // width, part, 0)


def head_stage(pairs, hidden, tables, partner):
    values = [hidden[r, c] for _, r, c in pairs]
    wide = [v.astype(F32) for v in values]
    scale = [lax.rsqrt(jnp.mean(x * x, axis=-1, keepdims=True) + 1e-06) for x in wide]
    normed = [x * s for x, s in zip(wide, scale)]
    turned = [swap_lanes(n, partner) for n in normed]
    queries = [split(n * tables[t, 0] + w * tables[t, 1]) for (t, _, _), n, w in zip(pairs, normed, turned)]
    keys = [split(n * tables[t, 2] + w * tables[t, 3]) for (t, _, _), n, w in zip(pairs, normed, turned)]
    scores = [
        nt(jnp.concatenate([qh, ql, qh], axis=1), jnp.concatenate([kh, kh, kl], axis=1))
        for (qh, ql), (kh, kl) in zip(queries, keys)
    ]
    raised = [jnp.exp(s) for s in scores]
    weights = [e * (1.0 / jnp.sum(e, axis=-1, keepdims=True)) for e in raised]
    return values, normed, scale, [q[0] for q in queries], [k[0] for k in keys], weights


def head_pairs(step, groups, tok, head, together):
    cols = [pl.ds(pl.multiple_of((step * together + u) * head, head), head) for u in range(together)]
    return [(t, slice(t * tok, (t + 1) * tok), c) for c in cols for t in range(groups)]


def mix_rows(hidden, tables, partner_ref, mixed, tok, head, together):
    groups = hidden.shape[0] // tok
    partner = partner_ref[...]

    def some(i, carry):
        pairs = head_pairs(i, groups, tok, head, together)
        values, _, _, _, _, weights = head_stage(pairs, hidden, tables, partner)
        rounded = [w.astype(BF16) for w in weights]
        results = [jnp.dot(w, v, preferred_element_type=F32).astype(BF16) for w, v in zip(rounded, values)]
        for (_, r, c), m in zip(pairs, results):
            mixed[r, c] = m
        return carry

    lax.fori_loop(0, hidden.shape[1] // head // together, some, 0)


def pull_rows(
    hidden, grad, grad_mixed, tables, cos_ref, sin_ref, first, gain, partner_ref, counts, sums, out, gain_out, tok, head, together
):
    groups = hidden.shape[0] // tok
    partner = partner_ref[...]
    sums[...] = jnp.zeros(sums.shape, F32)

    def some(i, carry):
        pairs = head_pairs(i, groups, tok, head, together)
        values, normed, scale, queries, keys, weights = head_stage(pairs, hidden, tables, partner)
        above = [grad_mixed[r, c] for _, r, c in pairs]
        grad_weights = [nt(a, v).astype(BF16).astype(F32) for a, v in zip(above, values)]
        if out is not None:
            grad_values = [tn(w.astype(BF16), a) for w, a in zip(weights, above)]
        means = [jnp.sum(g * w, axis=-1, keepdims=True) for g, w in zip(grad_weights, weights)]
        grad_scores = [(w * (g - m)).astype(BF16) for w, g, m in zip(weights, grad_weights, means)]
        grad_q = [jnp.dot(s, k, preferred_element_type=F32) for s, k in zip(grad_scores, keys)]
        grad_k = [tn(s, q) for s, q in zip(grad_scores, queries)]
        swap_q = [swap_lanes(g, partner) for g in grad_q]
        swap_k = [swap_lanes(g, partner) for g in grad_k]
        back_q = [g * cos_ref[first + p[0]] - w * sin_ref[first + p[0]] for p, g, w in zip(pairs, grad_q, swap_q)]
        back_k = [g * cos_ref[first + p[0]] - w * sin_ref[first + p[0]] for p, g, w in zip(pairs, grad_k, swap_k)]
        for t in range(groups):
            mine = [j for j, p in enumerate(pairs) if p[0] == t]
            sums[t, 0] += sum(normed[j] * back_q[j] for j in mine)
            sums[t, 1] += sum(normed[j] * back_k[j] for j in mine)
        if out is not None:
            grad_normed = [q * gain[0:1] + k * gain[2:3] for q, k in zip(back_q, back_k)]
            along = [jnp.mean(n * g, axis=-1, keepdims=True) for n, g in zip(normed, grad_normed)]
            grad_hidden = [
                (v + s * (g - n * a)).astype(BF16).astype(F32)
                for v, s, g, n, a in zip(grad_values, scale, grad_normed, normed, along)
            ]
            for (_, r, c), g in zip(pairs, grad_hidden):
                out[r, c] = (grad[r, c].astype(F32) + g).astype(BF16)
        return carry

    lax.fori_loop(0, hidden.shape[1] // head // together, some, 0)
    factor = 1.0 / math.sqrt(head)
    total_q = sum(counts[t].astype(F32) * jnp.sum(sums[t, 0], axis=0, keepdims=True) for t in range(groups))
    total_k = sum(counts[t].astype(F32) * jnp.sum(sums[t, 1], axis=0, keepdims=True) for t in range(groups))
    gain_out[...] = jnp.concatenate(
        [total_q * factor, total_k, jnp.zeros((gain_out.shape[0] - 2, head), F32)], axis=0
    )


def params(flops, size):
    return dict(
        compiler_params=pltpu.CompilerParams(vmem_limit_bytes=VMEM_BYTES),
        cost_estimate=pl.CostEstimate(flops=flops, bytes_accessed=size, transcendentals=0),
    )


IN_VMEM = pl.BlockSpec(memory_space=pltpu.VMEM)
IN_SMEM = pl.BlockSpec(memory_space=pltpu.SMEM)
ANYWHERE = pl.BlockSpec(memory_space=pl.ANY)


class Plan:
    def __init__(self, clips, out_proj, qk_gains):
        self.depth = lax.axis_size("pipe")
        self.ways = lax.axis_size("dp")
        self.tok = clips.shape[2]
        self.channels = clips.shape[3]
        self.head = qk_gains.shape[-1]
        self.heads = self.channels // self.head
        self.tiles = clips.shape[0] * clips.shape[1]
        self.rows = out_proj.shape[1]
        self.share = self.tiles * self.tok // self.depth
        self.held = max(-(-(p * self.share % self.tok + self.share) // self.tok) for p in range(self.depth))
        self.span = self.held * self.tok
        self.width = math.gcd(self.channels, 512)
        self.chips = self.ways // CORES


def mix_kernel(hidden, cos_ref, sin_ref, gains, partner_ref, mixed, tables, *, plan):
    fill_tables(tables, cos_ref, sin_ref, gains.at[0])
    mix_rows(hidden, tables, partner_ref, mixed, plan.tok, plan.head, plan.heads)


def first_mix(plan, rows, cos, sin, gains, partner):
    pair = CORES
    block = pl.BlockSpec((pair * plan.tok, plan.channels), lambda i: (i, 0))
    angle = pl.BlockSpec((pair, plan.tok, plan.head), lambda i: (i, 0, 0))
    whole = lambda x: pl.BlockSpec(x.shape, lambda i: (0,) * x.ndim)
    return pl.pallas_call(
        functools.partial(mix_kernel, plan=plan),
        grid=(plan.tiles // pair,),
        out_shape=jax.ShapeDtypeStruct(rows.shape, BF16),
        in_specs=[block, angle, angle, whole(gains), whole(partner)],
        out_specs=block,
        scratch_shapes=[pltpu.VMEM((pair, 4, plan.tok, plan.head), F32)],
        name="first_mix",
        **params(4 * rows.size * plan.tok * 4, 4 * rows.size),
    )(rows, cos, sin, gains, partner)


def weight_copies(plan, scalars, blocks, phase, buffer, sems):
    start = pl.multiple_of(scalars[plan.ways + phase], math.gcd(plan.rows, 16))
    return [
        pltpu.make_async_copy(
            block.at[pl.ds(start, plan.rows)],
            buffer.at[pl.ds(pl.multiple_of(scalars[i], math.gcd(plan.rows, 16)), plan.rows)],
            sems.at[i],
        )
        for i, block in enumerate(blocks)
    ]


def chain_kernel(scalars, *refs, plan):
    blocks, refs = refs[: plan.ways], refs[plan.ways :]
    rows, mixed_first, cotangent, cos_ref, sin_ref, gains, partner_ref = refs[:7]
    states, sent, grad_out, grad_sent, gain_out = refs[7:12]
    buffer, start, mixed, grad_in, grad_mixed, tables, sums, sems, row_sems = refs[12:]
    last = plan.depth - 1
    base = scalars[plan.ways + plan.depth]
    window = pl.multiple_of(scalars[plan.ways + plan.depth + 1], math.gcd(plan.share, plan.tok))
    counts = [scalars[plan.ways + plan.depth + 2 + t] for t in range(plan.held)]
    own = pl.ds(pl.multiple_of(base * plan.tok, plan.tok), plan.span)
    loads = [
        pltpu.make_async_copy(source.at[own], target, row_sems.at[i])
        for i, (source, target) in enumerate(((rows, start), (mixed_first, mixed), (cotangent, grad_in)))
    ]
    for load in loads:
        load.start()

    def fetch(phase):
        copies = weight_copies(plan, scalars, blocks, phase, buffer.at[phase % 2], sems.at[phase % 2])
        for copy in copies:
            copy.start()
        return copies

    coming = {phase: fetch(phase) for phase in range(min(2, plan.depth))}
    for load in loads:
        load.wait()
    hidden = start
    for phase in range(plan.depth):
        if phase:
            fill_tables(tables, cos_ref, sin_ref, gains.at[phase], base)
            mix_rows(hidden, tables, partner_ref, mixed, plan.tok, plan.head, plan.heads)
            sent[phase - 1] = mixed[pl.ds(window, plan.share), :]
        for copy in coming[phase]:
            copy.wait()
        if phase < last:
            project(hidden, mixed, buffer.at[phase % 2], states.at[phase], plan.width)
            hidden = states.at[phase]
            if phase + 2 <= last:
                coming[phase + 2] = fetch(phase + 2)
    pull_mixed(grad_in, buffer.at[last % 2], grad_mixed, plan.width)
    pull_rows(
        hidden, grad_in, grad_mixed, tables, cos_ref, sin_ref, base, gains.at[last], partner_ref, counts, sums,
        grad_out, gain_out, plan.tok, plan.head, plan.heads,
    )
    grad_sent[...] = grad_out[pl.ds(window, plan.share), :]


def chain(plan, scalars, blocks, rows, mixed_first, cotangent, cos, sin, gains, partner):
    shape = jax.ShapeDtypeStruct
    return pl.pallas_call(
        functools.partial(chain_kernel, plan=plan),
        out_shape=(
            shape((plan.depth - 1, plan.span, plan.channels), BF16),
            shape((plan.depth - 1, plan.share, plan.channels), BF16),
            shape((plan.span, plan.channels), BF16),
            shape((plan.share, plan.channels), BF16),
            shape((8, plan.head), F32),
        ),
        in_specs=[IN_SMEM] + [ANYWHERE] * (plan.ways + 3) + [IN_VMEM] * 4,
        out_specs=(IN_VMEM,) * 5,
        scratch_shapes=[
            pltpu.VMEM((2, plan.channels, plan.channels), BF16),
            pltpu.VMEM((plan.span, plan.channels), BF16),
            pltpu.VMEM((plan.span, plan.channels), BF16),
            pltpu.VMEM((plan.span, plan.channels), BF16),
            pltpu.VMEM((plan.span, plan.channels), BF16),
            pltpu.VMEM((plan.held, 4, plan.tok, plan.head), F32),
            pltpu.VMEM((plan.held, 2, plan.tok, plan.head), F32),
            pltpu.SemaphoreType.DMA((2, plan.ways)),
            pltpu.SemaphoreType.DMA((3,)),
        ],
        name="chain",
        **params(2 * plan.depth * plan.span * plan.channels * plan.channels * 2, 2 * plan.depth * plan.channels**2),
    )(scalars, *blocks, rows, mixed_first, cotangent, cos, sin, gains, partner)


def back_kernel(scalars, *refs, plan, phase):
    blocks, refs = refs[: plan.ways], refs[plan.ways :]
    hidden_any, grad_in, cos_ref, sin_ref, gains, partner_ref = refs[:6]
    if phase:
        grad_out, grad_sent, gain_out = refs[6:9]
        refs = refs[9:]
    else:
        grad_out, gain_out = None, refs[6]
        refs = refs[7:]
    buffer, hidden, grad_mixed, tables, sums, sems, row_sem = refs
    base = scalars[plan.ways + plan.depth]
    window = pl.multiple_of(scalars[plan.ways + plan.depth + 1], math.gcd(plan.share, plan.tok))
    counts = [scalars[plan.ways + plan.depth + 2 + t] for t in range(plan.held)]
    copies = weight_copies(plan, scalars, blocks, phase, buffer, sems)
    for copy in copies:
        copy.start()
    if phase:
        source = hidden_any.at[phase - 1]
    else:
        source = hidden_any.at[pl.ds(pl.multiple_of(base * plan.tok, plan.tok), plan.span)]
    load = pltpu.make_async_copy(source, hidden, row_sem.at[0])
    load.start()
    fill_tables(tables, cos_ref, sin_ref, gains.at[phase], base)
    for copy in copies:
        copy.wait()
    pull_mixed(grad_in, buffer, grad_mixed, plan.width)
    load.wait()
    pull_rows(
        hidden, grad_in, grad_mixed, tables, cos_ref, sin_ref, base, gains.at[phase], partner_ref, counts, sums,
        grad_out, gain_out, plan.tok, plan.head, plan.heads,
    )
    if phase:
        grad_sent[...] = grad_out[pl.ds(window, plan.share), :]


def back(plan, phase, scalars, blocks, hidden, grad_in, cos, sin, gains, partner):
    shape = jax.ShapeDtypeStruct
    grads = (shape((plan.span, plan.channels), BF16), shape((plan.share, plan.channels), BF16)) if phase else ()
    return pl.pallas_call(
        functools.partial(back_kernel, plan=plan, phase=phase),
        out_shape=grads + (shape((8, plan.head), F32),),
        in_specs=[IN_SMEM] + [ANYWHERE] * (plan.ways + 1) + [IN_VMEM] * 5,
        out_specs=(IN_VMEM,) * (len(grads) + 1),
        scratch_shapes=[
            pltpu.VMEM((plan.channels, plan.channels), BF16),
            pltpu.VMEM((plan.span, plan.channels), BF16),
            pltpu.VMEM((plan.span, plan.channels), BF16),
            pltpu.VMEM((plan.held, 4, plan.tok, plan.head), F32),
            pltpu.VMEM((plan.held, 2, plan.tok, plan.head), F32),
            pltpu.SemaphoreType.DMA((plan.ways,)),
            pltpu.SemaphoreType.DMA((1,)),
        ],
        name="back",
        **params(6 * plan.span * plan.channels * plan.channels, 3 * plan.channels**2),
    )(scalars, *blocks, hidden, grad_in, cos, sin, gains, partner)


def turn_kernel(place, *refs, plan):
    own, mixed_first, received = refs[0], refs[1], refs[2 : plan.depth + 1]
    out, gathered, sems = refs[plan.depth + 1 :]
    me = place[0]

    def gather(first):
        copies = []
        for k in range(plan.depth):
            if first:
                source = mixed_first.at[pl.ds(k * plan.share, plan.share)]
            elif k:
                source = received[k - 1]
            else:
                source = own.at[jnp.maximum(me, 1) - 1]
            copies.append(pltpu.make_async_copy(source, gathered.at[pl.ds(k * plan.share, plan.share)], sems.at[k]))
        for copy in copies:
            copy.start()
        for copy in copies:
            copy.wait()

    pl.when(me == 0)(lambda: gather(True))
    pl.when(me != 0)(lambda: gather(False))

    def part(i, carry):
        cols = pl.ds(pl.multiple_of(i * plan.width, plan.width), plan.width)
        out[cols, :] = gathered[:, cols].T
        return carry

    lax.fori_loop(0, plan.channels // plan.width, part, 0)


def turn(plan, place, own, mixed_first, received):
    total = plan.depth * plan.share
    return pl.pallas_call(
        functools.partial(turn_kernel, plan=plan),
        out_shape=jax.ShapeDtypeStruct((plan.channels, total), BF16),
        in_specs=[IN_SMEM] + [ANYWHERE] * (plan.depth + 1),
        out_specs=IN_VMEM,
        scratch_shapes=[pltpu.VMEM((total, plan.channels), BF16), pltpu.SemaphoreType.DMA((plan.depth,))],
        name="turn",
        **params(0, 4 * total * plan.channels),
    )(place, own, mixed_first, *received)


def term_kernel(place, *refs, plan, theirs):
    turned, cotangent, refs = refs[0], refs[1], refs[2:]
    sources = [refs[i * plan.depth : (i + 1) * plan.depth] for i in range(plan.depth - 1)]
    refs = refs[plan.depth * (plan.depth - 1) :]
    if theirs:
        out, grads, sems = refs
    else:
        partial, out, grads, sems = refs
    me, core = place[0], place[1]

    def gather(phase):
        copies = []
        for k in range(plan.depth):
            if phase == plan.depth - 1:
                source = cotangent.at[pl.ds((phase ^ k) * plan.share, plan.share)]
            else:
                source = sources[phase][k]
            copies.append(pltpu.make_async_copy(source, grads.at[pl.ds(k * plan.share, plan.share)], sems.at[k]))
        for copy in copies:
            copy.start()
        for copy in copies:
            copy.wait()

    for phase in range(plan.depth):
        pl.when(me == phase)(functools.partial(gather, phase))
    which = 1 - core if theirs else core

    def part(chip, carry):
        here = pl.multiple_of((chip * CORES + which) * plan.rows, math.gcd(plan.rows, 16))
        term = jnp.dot(turned[pl.ds(here, plan.rows), :], grads[...], preferred_element_type=F32)
        if not theirs:
            term = term + partial[chip].astype(F32)
        out[chip] = term.astype(BF16)
        return carry

    lax.fori_loop(0, plan.chips, part, 0)


def term(plan, place, turned, cotangent, sources, partial=None):
    total = plan.depth * plan.share
    flat = [x for phase in sources for x in phase]
    extra = [] if partial is None else [partial]
    return pl.pallas_call(
        functools.partial(term_kernel, plan=plan, theirs=partial is None),
        out_shape=jax.ShapeDtypeStruct((plan.chips, plan.rows, plan.channels), BF16),
        in_specs=[IN_SMEM, IN_VMEM] + [ANYWHERE] * (1 + len(flat)) + [IN_VMEM] * len(extra),
        out_specs=IN_VMEM,
        scratch_shapes=[pltpu.VMEM((total, plan.channels), BF16), pltpu.SemaphoreType.DMA((plan.depth,))],
        name="term",
        **params(total * plan.channels**2, 4 * plan.channels**2),
    )(place, turned, cotangent, *flat, *extra)


def along_pipe(x, k):
    return lax.ppermute(x, "pipe", [(i, i ^ k) for i in range(lax.axis_size("pipe"))])


def to_place(x, k, place):
    return lax.ppermute(x, "pipe", [(place ^ k, place)])


def along_chips(x, k):
    return lax.ppermute(x, "dp", [(i, i ^ (CORES * k)) for i in range(lax.axis_size("dp"))])


def other_core(x):
    return lax.ppermute(x, "dp", [(i, i ^ 1) for i in range(lax.axis_size("dp"))])


def spread_near(block, depth):
    return {1 << bit: along_pipe(block, 1 << bit) for bit in range(depth.bit_length() - 1)}


def spread_far(block, near, depth):
    bits = depth.bit_length() - 1
    part = block.shape[0] // max(bits, 1)
    got = {0: block, **near}
    for k in sorted(range(1, depth), key=lambda k: k.bit_count()):
        if k in got:
            continue
        pieces = []
        for i in range(bits):
            order = [(i + b) % bits for b in range(bits)]
            bit = [b for b in order if k >> b & 1][-1]
            pieces.append(along_pipe(got[k ^ (1 << bit)][i * part : (i + 1) * part], 1 << bit))
        got[k] = jnp.concatenate(pieces, axis=0)
    return [got[k] for k in range(depth)]


def gather_weights(plan, own, chip):
    chips = plan.chips
    order = [sorted((b for b in range(chips) if b != c), key=lambda b: (abs(b - c), b ^ c)) for c in range(chips)]
    up = down = block = own
    arrived = {}
    stacks, whose = [], []
    for step in range(1, chips + 1):
        near = spread_near(block, plan.depth)
        if step < chips:
            up = lax.ppermute(up, "dp", [(i, i + CORES) for i in range(plan.ways - CORES)])
            down = lax.ppermute(down, "dp", [(i + CORES, i) for i in range(plan.ways - CORES)])
            keys = list(near)
            up, down, *held = lax.optimization_barrier((up, down, *near.values()))
            near = dict(zip(keys, held))
            arrived[step, -1], arrived[step, 1] = up, down
        stacks.append(jnp.concatenate(spread_far(block, near, plan.depth), axis=0))
        source = [c if step == 1 else order[c][step - 2] for c in range(chips)]
        whose.append(jnp.asarray(source, jnp.int32)[chip])
        if step < chips:
            places = {}
            for c in range(chips):
                b = order[c][step - 1]
                places.setdefault((abs(b - c), 1 if b > c else -1), []).append(c)
            (first, _), *others = places.items()
            block = arrived[first]
            for key, members in others:
                here = functools.reduce(jnp.logical_or, [chip == c for c in members])
                block = jnp.where(here, arrived[key], block)
    return stacks, whose


def shards(clips, positions, out_proj, qk_gains, cotangent):
    plan = Plan(clips, out_proj, qk_gains)
    depth, last = plan.depth, plan.depth - 1
    place = lax.axis_index("pipe")
    member = lax.axis_index("dp")
    chip, core = member // CORES, member % CORES

    stacks, whose = gather_weights(plan, out_proj[0], chip)
    blocks = stacks + [other_core(stack) for stack in stacks]
    starts = [(w * CORES + core) * plan.rows for w in whose] + [(w * CORES + 1 - core) * plan.rows for w in whose]

    first_row = place * plan.share
    base = jnp.minimum(first_row // plan.tok, plan.tiles - plan.held)
    tile_starts = [(base + t) * plan.tok for t in range(plan.held)]
    counts = [((s >= first_row) & (s < first_row + plan.share)).astype(jnp.int32) for s in tile_starts]
    scalars = jnp.stack(
        starts + [(place ^ s) * plan.rows for s in range(depth)] + [base, first_row - base * plan.tok] + counts
    ).astype(jnp.int32)

    coord, freq, sign, partner = lane_tables(plan.head)
    spots = positions.reshape(3, plan.tiles, plan.tok, 1).astype(F32)
    angles = jnp.where(coord == 0, spots[0], jnp.where(coord == 1, spots[1], spots[2])) * freq
    cos, sin = jnp.cos(angles), jnp.sin(angles) * sign
    gain_table = lax.all_gather(qk_gains[0], "pipe").astype(F32)
    factor = 1.0 / math.sqrt(plan.head)
    swapped = gain_table[..., partner]
    queries, keys = gain_table[:, 0] * factor, gain_table[:, 1]
    rows_of = [queries, swapped[:, 0] * factor, keys, swapped[:, 1]]
    gains = jnp.stack(rows_of + [jnp.zeros_like(keys)] * 4, axis=1)
    partners = jnp.broadcast_to(jnp.asarray(partner), (plan.tok, plan.head))
    setting = (cos, sin, gains, partners)

    rows = clips.reshape(plan.tiles * plan.tok, plan.channels)
    last_grad = cotangent.reshape(plan.tiles * plan.tok, plan.channels)
    mixed_first = first_mix(plan, rows, *setting)
    states, mixed, grad, grad_window, gain = chain(plan, scalars, blocks, rows, mixed_first, last_grad, *setting)
    gain_terms = {last: gain}
    sources = {}
    received = []
    for k in range(1, depth):
        chosen = lax.dynamic_index_in_dim(mixed, jnp.maximum(place ^ k, 1) - 1, 0, keepdims=False)
        pairs = [(i, i ^ k) for i in range(depth) if i ^ k]
        received.append(lax.ppermute(chosen, "pipe", pairs))
    for phase in range(last - 1, -1, -1):
        sources[phase] = [grad_window] + [to_place(grad_window, k, phase) for k in range(1, depth)]
        if phase:
            grad, grad_window, gain = back(plan, phase, scalars, blocks, states, grad, *setting)
        else:
            (gain,) = back(plan, phase, scalars, blocks, rows, grad, *setting)
        gain_terms[phase] = gain

    where = jnp.stack([place, core]).astype(jnp.int32)
    turned = turn(plan, where, mixed, mixed_first, received)
    flat = [sources[phase] for phase in range(last)]
    theirs = term(plan, where, turned, last_grad, flat)
    mine = term(plan, where, turned, last_grad, flat, other_core(theirs))
    total = lax.dynamic_index_in_dim(mine, chip, 0, keepdims=False).astype(F32)
    for k in range(1, plan.chips):
        piece = lax.dynamic_index_in_dim(mine, chip ^ k, 0, keepdims=False)
        total = total + along_chips(piece, k).astype(F32)

    gain_sums = lax.psum(jnp.stack([gain_terms[s][:2] for s in range(depth)]), ("pipe", "dp"))
    own_gains = lax.dynamic_index_in_dim(gain_sums, place, 0, keepdims=False)
    return (total[None], own_gains[None])


def solution(mesh):
    placed = (
        P(None, None, "dp", None),
        P(None, None, None, "dp"),
        P("pipe", "dp", None),
        P("pipe", None, None),
        P(None, None, "dp", None),
    )
    return jax.shard_map(
        shards,
        mesh=mesh,
        in_specs=placed,
        out_specs=(P("pipe", "dp", None), P("pipe", None, None)),
        check_vma=False,
    )
```

```python
import functools
import math

import jax
import jax.numpy as jnp
import numpy as np
from jax import lax
from jax.experimental import pallas as pl
from jax.experimental.pallas import tpu as pltpu
from jax.sharding import PartitionSpec as P

F32 = jnp.float32
BF16 = jnp.bfloat16
VMEM_BYTES = 56 * 1024 * 1024
CORES = 2
GAIN_ROWS = 8


def lane_tables(head):
    first = head // 8
    rest = (head - first) // 2
    coord = np.zeros(head, np.int32)
    freq = np.zeros(head, np.float32)
    sign = np.zeros(head, np.float32)
    partner = np.zeros(head, np.int32)
    offset = 0
    for axis, width in enumerate((first, rest, rest)):
        half = width // 2
        for j in range(half):
            low, high = offset + j, offset + j + half
            coord[low] = coord[high] = axis
            freq[low] = freq[high] = 256.0 ** (-2.0 * j / width)
            sign[low], sign[high] = -1.0, 1.0
            partner[low], partner[high] = high, low
        offset += width
    return coord, freq, sign, partner


def swap_lanes(x, partner):
    return jnp.take_along_axis(x, partner, axis=1, mode="promise_in_bounds")


def nt(a, b):
    return lax.dot_general(a, b, (((1,), (1,)), ((), ())), preferred_element_type=F32)


def tn(a, b):
    return lax.dot_general(a, b, (((0,), (0,)), ((), ())), preferred_element_type=F32)


def split(x):
    high = x.astype(BF16)
    return high, (x - high.astype(F32)).astype(BF16)


def fill_tables(tables, cos_ref, sin_ref, gain_ref, partner_ref, first=0):
    gain = gain_ref[...]
    turned = swap_lanes(gain, partner_ref[0 : gain.shape[0], :])
    factor = 1.0 / math.sqrt(gain.shape[-1])
    for t in range(tables.shape[0]):
        cosine, sine = cos_ref[first + t], sin_ref[first + t]
        tables[t, 0] = cosine * (gain[0:1] * factor)
        tables[t, 1] = sine * (turned[0:1] * factor)
        tables[t, 2] = cosine * gain[1:2]
        tables[t, 3] = sine * turned[1:2]


def project(hidden, mixed, weight, out, width):
    def part(i, carry):
        cols = pl.ds(pl.multiple_of(i * width, width), width)
        update = jnp.dot(mixed[...], weight[:, cols], preferred_element_type=F32)
        out[:, cols] = (hidden[:, cols].astype(F32) + update).astype(BF16)
        return carry

    lax.fori_loop(0, out.shape[1] // width, part, 0)


def pull_mixed(grad, weight, grad_mixed, width):
    def part(i, carry):
        cols = pl.ds(pl.multiple_of(i * width, width), width)
        grad_mixed[:, cols] = nt(grad[...], weight[cols, :]).astype(BF16)
        return carry

    lax.fori_loop(0, grad_mixed.shape[1] // width, part, 0)


def head_stage(pairs, hidden, tables, partner):
    values = [hidden[r, c] for _, r, c in pairs]
    wide = [v.astype(F32) for v in values]
    scale = [lax.rsqrt(jnp.mean(x * x, axis=-1, keepdims=True) + 1e-06) for x in wide]
    normed = [x * s for x, s in zip(wide, scale)]
    turned = [swap_lanes(n, partner) for n in normed]
    queries = [split(n * tables[t, 0] + w * tables[t, 1]) for (t, _, _), n, w in zip(pairs, normed, turned)]
    keys = [split(n * tables[t, 2] + w * tables[t, 3]) for (t, _, _), n, w in zip(pairs, normed, turned)]
    scores = [
        nt(jnp.concatenate([qh, ql, qh], axis=1), jnp.concatenate([kh, kh, kl], axis=1))
        for (qh, ql), (kh, kl) in zip(queries, keys)
    ]
    raised = [jnp.exp(s) for s in scores]
    weights = [e * (1.0 / jnp.sum(e, axis=-1, keepdims=True)) for e in raised]
    return values, normed, scale, [q[0] for q in queries], [k[0] for k in keys], weights


def head_pairs(step, groups, tok, head, together):
    cols = [pl.ds(pl.multiple_of((step * together + u) * head, head), head) for u in range(together)]
    return [(t, slice(t * tok, (t + 1) * tok), c) for c in cols for t in range(groups)]


def mix_rows(hidden, tables, partner_ref, mixed, tok, head, together):
    groups = hidden.shape[0] // tok
    partner = partner_ref[...]

    def some(i, carry):
        pairs = head_pairs(i, groups, tok, head, together)
        values, _, _, _, _, weights = head_stage(pairs, hidden, tables, partner)
        rounded = [w.astype(BF16) for w in weights]
        results = [jnp.dot(w, v, preferred_element_type=F32).astype(BF16) for w, v in zip(rounded, values)]
        for (_, r, c), m in zip(pairs, results):
            mixed[r, c] = m
        return carry

    lax.fori_loop(0, hidden.shape[1] // head // together, some, 0)


def pull_rows(
    hidden, grad, grad_mixed, tables, cos_ref, sin_ref, first, gain_ref, partner_ref, counts, sums, out, tok, head, together
):
    groups = hidden.shape[0] // tok
    partner = partner_ref[...]
    factor = 1.0 / math.sqrt(head)
    gain_q, gain_k = gain_ref[0:1, :] * factor, gain_ref[1:2, :]
    sums[...] = jnp.zeros(sums.shape, F32)

    def some(i, carry):
        pairs = head_pairs(i, groups, tok, head, together)
        values, normed, scale, queries, keys, weights = head_stage(pairs, hidden, tables, partner)
        above = [grad_mixed[r, c] for _, r, c in pairs]
        grad_weights = [nt(a, v).astype(BF16).astype(F32) for a, v in zip(above, values)]
        if out is not None:
            grad_values = [tn(w.astype(BF16), a) for w, a in zip(weights, above)]
        means = [jnp.sum(g * w, axis=-1, keepdims=True) for g, w in zip(grad_weights, weights)]
        grad_scores = [(w * (g - m)).astype(BF16) for w, g, m in zip(weights, grad_weights, means)]
        grad_q = [jnp.dot(s, k, preferred_element_type=F32) for s, k in zip(grad_scores, keys)]
        grad_k = [tn(s, q) for s, q in zip(grad_scores, queries)]
        swap_q = [swap_lanes(g, partner) for g in grad_q]
        swap_k = [swap_lanes(g, partner) for g in grad_k]
        back_q = [g * cos_ref[first + p[0]] - w * sin_ref[first + p[0]] for p, g, w in zip(pairs, grad_q, swap_q)]
        back_k = [g * cos_ref[first + p[0]] - w * sin_ref[first + p[0]] for p, g, w in zip(pairs, grad_k, swap_k)]
        for t in range(groups):
            mine = [j for j, p in enumerate(pairs) if p[0] == t]
            sums[t, 0] += sum(normed[j] * back_q[j] for j in mine)
            sums[t, 1] += sum(normed[j] * back_k[j] for j in mine)
        if out is not None:
            grad_normed = [q * gain_q + k * gain_k for q, k in zip(back_q, back_k)]
            along = [jnp.mean(n * g, axis=-1, keepdims=True) for n, g in zip(normed, grad_normed)]
            grad_hidden = [
                (v + s * (g - n * a)).astype(BF16).astype(F32)
                for v, s, g, n, a in zip(grad_values, scale, grad_normed, normed, along)
            ]
            for (_, r, c), g in zip(pairs, grad_hidden):
                out[r, c] = (grad[r, c].astype(F32) + g).astype(BF16)
        return carry

    lax.fori_loop(0, hidden.shape[1] // head // together, some, 0)
    total = [
        sum(counts[t] * jnp.sum(sums[t, i], axis=0, keepdims=True) for t in range(groups)) for i in range(2)
    ]
    return jnp.concatenate([total[0] * factor, total[1], jnp.zeros((GAIN_ROWS - 2, head), F32)], axis=0)


def params(flops, size):
    return dict(
        compiler_params=pltpu.CompilerParams(vmem_limit_bytes=VMEM_BYTES),
        cost_estimate=pl.CostEstimate(flops=flops, bytes_accessed=size, transcendentals=0),
    )


IN_VMEM = pl.BlockSpec(memory_space=pltpu.VMEM)
IN_SMEM = pl.BlockSpec(memory_space=pltpu.SMEM)
ANYWHERE = pl.BlockSpec(memory_space=pl.ANY)


class Plan:
    def __init__(self, clips, out_proj, qk_gains):
        self.depth = lax.axis_size("pipe")
        self.ways = lax.axis_size("dp")
        self.tok = clips.shape[2]
        self.channels = clips.shape[3]
        self.head = qk_gains.shape[-1]
        self.heads = self.channels // self.head
        self.tiles = clips.shape[0] * clips.shape[1]
        self.rows = out_proj.shape[1]
        self.share = self.tiles * self.tok // self.depth
        self.held = max(-(-(p * self.share % self.tok + self.share) // self.tok) for p in range(self.depth))
        self.span = self.held * self.tok
        self.width = math.gcd(self.channels, 512)
        self.chips = self.ways // CORES
        self.phase_at = self.ways
        self.base_at = self.ways + self.depth
        self.window_at = self.base_at + 1
        self.place_at = self.base_at + 2
        self.counts_at = self.base_at + 3


def weight_copies(plan, scalars, blocks, phase, buffer, sems):
    start = pl.multiple_of(scalars[plan.phase_at + phase], math.gcd(plan.rows, 16))
    return [
        pltpu.make_async_copy(
            block.at[pl.ds(start, plan.rows)],
            buffer.at[pl.ds(pl.multiple_of(scalars[i], math.gcd(plan.rows, 16)), plan.rows)],
            sems.at[i],
        )
        for i, block in enumerate(blocks)
    ]


def window_of(plan, scalars):
    return pl.ds(pl.multiple_of(scalars[plan.window_at], math.gcd(plan.share, plan.tok)), plan.share)


def own_rows(plan, scalars):
    return pl.ds(pl.multiple_of(scalars[plan.base_at] * plan.tok, plan.tok), plan.span)


def forward_kernel(scalars, *refs, plan):
    blocks, refs = refs[: plan.ways], refs[plan.ways :]
    rows, cos_ref, sin_ref, gains, partner_ref = refs[:5]
    states, sent = refs[5:7]
    buffer, start, mixed, tables, sems, row_sem = refs[7:]
    last = plan.depth - 1
    base = scalars[plan.base_at]
    load = pltpu.make_async_copy(rows.at[own_rows(plan, scalars)], start, row_sem.at[0])
    load.start()

    def fetch(phase):
        copies = weight_copies(plan, scalars, blocks, phase, buffer.at[phase % 2], sems.at[phase % 2])
        for copy in copies:
            copy.start()
        return copies

    coming = {phase: fetch(phase) for phase in range(min(2, last))}
    for phase in range(plan.depth):
        hidden = states.at[phase - 1] if phase else start
        fill_tables(tables, cos_ref, sin_ref, gains.at[phase], partner_ref, base)
        if phase == 0:
            load.wait()
        mix_rows(hidden, tables, partner_ref, mixed, plan.tok, plan.head, plan.heads)
        sent[phase] = mixed[window_of(plan, scalars), :]
        if phase < last:
            for copy in coming[phase]:
                copy.wait()
            project(hidden, mixed, buffer.at[phase % 2], states.at[phase], plan.width)
            if phase + 2 < last:
                coming[phase + 2] = fetch(phase + 2)


def forward(plan, scalars, blocks, rows, cos, sin, gains, partner):
    shape = jax.ShapeDtypeStruct
    return pl.pallas_call(
        functools.partial(forward_kernel, plan=plan),
        out_shape=(
            shape((plan.depth - 1, plan.span, plan.channels), BF16),
            shape((plan.depth, plan.share, plan.channels), BF16),
        ),
        in_specs=[IN_SMEM] + [ANYWHERE] * (plan.ways + 1) + [IN_VMEM] * 4,
        out_specs=(IN_VMEM,) * 2,
        scratch_shapes=[
            pltpu.VMEM((2, plan.channels, plan.channels), BF16),
            pltpu.VMEM((plan.span, plan.channels), BF16),
            pltpu.VMEM((plan.span, plan.channels), BF16),
            pltpu.VMEM((plan.held, 4, plan.tok, plan.head), F32),
            pltpu.SemaphoreType.DMA((2, plan.ways)),
            pltpu.SemaphoreType.DMA((1,)),
        ],
        name="forward",
        **params(2 * plan.depth * plan.span * plan.channels * plan.channels, 2 * plan.depth * plan.channels**2),
    )(scalars, *blocks, rows, cos, sin, gains, partner)


def back_kernel(scalars, *refs, plan, phase):
    blocks, refs = refs[: plan.ways], refs[plan.ways :]
    hidden_any, grad_any, cos_ref, sin_ref, gains, partner_ref = refs[:6]
    if phase:
        grad_out, grad_sent, gain_out = refs[6:9]
    else:
        grad_out, gain_out = None, refs[6]
    buffer, hidden, grad_in, grad_mixed, tables, sums, sems, row_sems = refs[-8:]
    base = scalars[plan.base_at]
    counts = [scalars[plan.counts_at + t].astype(F32) for t in range(plan.held)]
    copies = weight_copies(plan, scalars, blocks, phase, buffer, sems)
    own = own_rows(plan, scalars)
    copies += [
        pltpu.make_async_copy(grad_any.at[own] if phase == plan.depth - 1 else grad_any, grad_in, row_sems.at[0]),
        pltpu.make_async_copy(hidden_any.at[phase - 1] if phase else hidden_any.at[own], hidden, row_sems.at[1]),
    ]
    for copy in copies:
        copy.start()
    fill_tables(tables, cos_ref, sin_ref, gains.at[phase], partner_ref, base)
    for copy in copies:
        copy.wait()
    pull_mixed(grad_in, buffer, grad_mixed, plan.width)
    gain_out[...] = pull_rows(
        hidden, grad_in, grad_mixed, tables, cos_ref, sin_ref, base, gains.at[phase], partner_ref, counts, sums,
        grad_out, plan.tok, plan.head, plan.heads,
    )
    if phase:
        grad_sent[...] = grad_out[window_of(plan, scalars), :]


def back(plan, phase, scalars, blocks, hidden, grad_in, cos, sin, gains, partner):
    shape = jax.ShapeDtypeStruct
    rows = pltpu.VMEM((plan.span, plan.channels), BF16)
    grads = (shape((plan.span, plan.channels), BF16), shape((plan.share, plan.channels), BF16)) if phase else ()
    return pl.pallas_call(
        functools.partial(back_kernel, plan=plan, phase=phase),
        out_shape=(*grads, shape((GAIN_ROWS, plan.head), F32)),
        in_specs=[IN_SMEM] + [ANYWHERE] * (plan.ways + 2) + [IN_VMEM] * 4,
        out_specs=(IN_VMEM,) * (len(grads) + 1),
        scratch_shapes=[
            pltpu.VMEM((plan.channels, plan.channels), BF16),
            rows,
            rows,
            rows,
            pltpu.VMEM((plan.held, 4, plan.tok, plan.head), F32),
            pltpu.VMEM((plan.held, 2, plan.tok, plan.head), F32),
            pltpu.SemaphoreType.DMA((plan.ways,)),
            pltpu.SemaphoreType.DMA((2,)),
        ],
        name="back",
        **params(6 * plan.span * plan.channels * plan.channels, 3 * plan.channels**2),
    )(scalars, *blocks, hidden, grad_in, cos, sin, gains, partner)


def turn_kernel(place, *refs, plan):
    own, received = refs[0], refs[1 : plan.depth]
    out, gathered, sems = refs[plan.depth :]
    copies = [
        pltpu.make_async_copy(
            received[k - 1] if k else own.at[place[0]], gathered.at[pl.ds(k * plan.share, plan.share)], sems.at[k]
        )
        for k in range(plan.depth)
    ]
    for copy in copies:
        copy.start()
    for copy in copies:
        copy.wait()

    def part(i, carry):
        cols = pl.ds(pl.multiple_of(i * plan.width, plan.width), plan.width)
        out[cols, :] = gathered[:, cols].T
        return carry

    lax.fori_loop(0, plan.channels // plan.width, part, 0)


def turn(plan, place, own, received):
    total = plan.depth * plan.share
    return pl.pallas_call(
        functools.partial(turn_kernel, plan=plan),
        out_shape=jax.ShapeDtypeStruct((plan.channels, total), BF16),
        in_specs=[IN_SMEM] + [ANYWHERE] * plan.depth,
        out_specs=IN_VMEM,
        scratch_shapes=[pltpu.VMEM((total, plan.channels), BF16), pltpu.SemaphoreType.DMA((plan.depth,))],
        name="turn",
        **params(0, 4 * total * plan.channels),
    )(place, own, *received)


def term_kernel(place, turned_any, cotangent, windows, *refs, plan, theirs):
    received, refs = refs[: plan.depth - 1], refs[plan.depth - 1 :]
    out, turned, grads, sems = refs
    me, core = place[0], place[1]
    load = pltpu.make_async_copy(turned_any, turned, sems.at[plan.depth])
    load.start()

    def gather(from_cotangent):
        for k in range(plan.depth):
            if from_cotangent:
                source = cotangent.at[pl.ds(((plan.depth - 1) ^ k) * plan.share, plan.share)]
            else:
                source = received[k - 1] if k else windows.at[jnp.minimum(me, plan.depth - 2)]
            pltpu.make_async_copy(source, grads.at[pl.ds(k * plan.share, plan.share)], sems.at[k]).start()

    pl.when(me == plan.depth - 1)(lambda: gather(True))
    pl.when(me != plan.depth - 1)(lambda: gather(False))
    for k in range(plan.depth):
        rows = pl.ds(k * plan.share, plan.share)
        pltpu.make_async_copy(cotangent.at[rows], grads.at[rows], sems.at[k]).wait()
    load.wait()
    which = 1 - core if theirs else core

    def part(chip, carry):
        here = pl.multiple_of((chip * CORES + which) * plan.rows, math.gcd(plan.rows, 16))
        term = jnp.dot(turned[pl.ds(here, plan.rows), :], grads[...], preferred_element_type=F32)
        out[chip] = term.astype(BF16)
        return carry

    lax.fori_loop(0, plan.chips, part, 0)


def term(plan, place, turned, cotangent, windows, received, theirs):
    total = plan.depth * plan.share
    return pl.pallas_call(
        functools.partial(term_kernel, plan=plan, theirs=theirs),
        out_shape=jax.ShapeDtypeStruct((plan.chips, plan.rows, plan.channels), BF16),
        in_specs=[IN_SMEM] + [ANYWHERE] * (2 + plan.depth),
        out_specs=IN_VMEM,
        scratch_shapes=[
            pltpu.VMEM((plan.channels, total), BF16),
            pltpu.VMEM((total, plan.channels), BF16),
            pltpu.SemaphoreType.DMA((plan.depth + 1,)),
        ],
        name="term",
        **params(total * plan.channels**2, 4 * plan.channels**2),
    )(place, turned, cotangent, windows, *received)


def along_pipe(x, k):
    return lax.ppermute(x, "pipe", [(i, i ^ k) for i in range(lax.axis_size("pipe"))])


def along_chips(x, k):
    return lax.ppermute(x, "dp", [(i, i ^ (CORES * k)) for i in range(lax.axis_size("dp"))])


def other_core(x):
    return lax.ppermute(x, "dp", [(i, i ^ 1) for i in range(lax.axis_size("dp"))])


def spread_near(block, depth):
    return {1 << bit: along_pipe(block, 1 << bit) for bit in range(depth.bit_length() - 1)}


def spread_far(block, near, depth):
    bits = depth.bit_length() - 1
    part = block.shape[0] // max(bits, 1)
    got = {k: [x[i * part : (i + 1) * part] for i in range(bits)] for k, x in near.items()}
    for k in sorted(range(1, depth), key=lambda k: k.bit_count()):
        if k not in got:
            got[k] = []
            for i in range(bits):
                order = [(i + b) % bits for b in range(bits)]
                bit = 1 << [b for b in order if k >> b & 1][-1]
                got[k].append(along_pipe(got[k ^ bit][i], bit))
    return {k: parts for k, parts in got.items() if k not in near}


def stacked(block, near, far, depth):
    pieces = []
    for k in range(depth):
        pieces += [block] if k == 0 else [near[k]] if k in near else far[k]
    return jnp.concatenate(pieces, axis=0)


def gather_weights(plan, own, gain, chip, beside):
    chips, depth = plan.chips, plan.depth
    order = [sorted((b for b in range(chips) if b != c), key=lambda b: (abs(b - c), b ^ c)) for c in range(chips)]
    up = down = block = own
    arrived = {}
    held, nears, fars, others, extra = [], [], [], [], ()
    gains, distance = gain[None], 1
    for step in range(1, chips + 1):
        held.append(block)
        near = spread_near(block, depth)
        more = ()
        if distance < depth:
            more = (along_pipe(gains, distance),)
            distance *= 2
        if step == 2:
            extra = beside()
        far = spread_far(held[-2], nears[-1], depth) if step > 1 else ()
        if step > 2:
            stack = stacked(held[step - 3], nears[step - 3], fars[step - 3], depth)
            others.append(other_core(stack))
        if step < chips:
            up = lax.ppermute(up, "dp", [(i, i + CORES) for i in range(plan.ways - CORES)])
            down = lax.ppermute(down, "dp", [(i + CORES, i) for i in range(plan.ways - CORES)])
        up, down, near, far, more, extra, others = lax.optimization_barrier(
            (up, down, near, far, more, extra, others)
        )
        nears.append(near)
        if step > 1:
            fars.append(far)
        arrived[step, -1], arrived[step, 1] = up, down
        gains = jnp.concatenate([gains, *more], axis=0)
        if step < chips:
            places = {}
            for c in range(chips):
                b = order[c][step - 1]
                places.setdefault((abs(b - c), 1 if b > c else -1), []).append(c)
            (first, _), *rest = places.items()
            block = arrived[first]
            for key, members in rest:
                here = functools.reduce(jnp.logical_or, [chip == c for c in members])
                block = jnp.where(here, arrived[key], block)
    fars.append(spread_far(held[-1], nears[-1], depth))
    while distance < depth:
        gains = jnp.concatenate([gains, along_pipe(gains, distance)], axis=0)
        distance *= 2
    stacks = [stacked(h, n, f, depth) for h, n, f in zip(held, nears, fars)]
    others += [other_core(stack) for stack in stacks[len(others) :]]
    whose = [jnp.asarray([c if i == 0 else order[c][i - 1] for c in range(chips)], jnp.int32)[chip] for i in range(chips)]
    return stacks, others, whose, gains, extra


def shards(clips, positions, out_proj, qk_gains, cotangent):
    plan = Plan(clips, out_proj, qk_gains)
    depth, last = plan.depth, plan.depth - 1
    place = lax.axis_index("pipe")
    member = lax.axis_index("dp")
    chip, core = member // CORES, member % CORES
    rows = clips.reshape(plan.tiles * plan.tok, plan.channels)
    last_grad = cotangent.reshape(plan.tiles * plan.tok, plan.channels)
    coord, freq, sign, partner = lane_tables(plan.head)
    partners = jnp.broadcast_to(jnp.asarray(partner), (plan.tok, plan.head))
    own_gain = jnp.pad(qk_gains[0], ((0, GAIN_ROWS - 2), (0, 0)))

    def angles():
        spots = positions.reshape(3, plan.tiles, plan.tok, 1).astype(F32)
        angle = jnp.where(coord == 0, spots[0], jnp.where(coord == 1, spots[1], spots[2])) * freq
        return jnp.cos(angle), jnp.sin(angle) * sign

    stacks, others, whose, gains, (cos, sin) = gather_weights(plan, out_proj[0], own_gain, chip, angles)
    blocks = stacks + others
    starts = [(w * CORES + core) * plan.rows for w in whose] + [(w * CORES + 1 - core) * plan.rows for w in whose]
    gains = gains[place ^ jnp.arange(depth)].astype(F32)
    setting = (cos, sin, gains, partners)

    first_row = place * plan.share
    base = jnp.minimum(first_row // plan.tok, plan.tiles - plan.held)
    tile_starts = [(base + t) * plan.tok for t in range(plan.held)]
    counts = [((t >= first_row) & (t < first_row + plan.share)).astype(jnp.int32) for t in tile_starts]
    offsets = [(place ^ s) * plan.rows for s in range(depth)]
    scalars = jnp.stack(starts + offsets + [base, first_row - base * plan.tok, place] + counts).astype(jnp.int32)

    def to_owners(windows):
        got = {}
        for k in range(1, depth):
            chosen = lax.dynamic_index_in_dim(windows, jnp.minimum(place ^ k, windows.shape[0] - 1), 0, keepdims=False)
            pairs = [(i, i ^ k) for i in range(depth) if i ^ k < windows.shape[0]]
            got[k] = lax.ppermute(chosen, "pipe", pairs)
        return got

    states, mixed = forward(plan, scalars, blocks, rows, *setting)
    received = to_owners(mixed)
    grad = last_grad
    gain_terms, windows = {}, {}
    for phase in range(last, 0, -1):
        grad, windows[phase - 1], gain_terms[phase] = back(plan, phase, scalars, blocks, states, grad, *setting)
        if phase == 2:
            near = {k: received[k] for k in received if k.bit_count() == 1}
            grad, near = lax.optimization_barrier((grad, near))
            received.update(near)
    windows = jnp.stack([windows[phase] for phase in range(last)])
    grads = to_owners(windows)
    (gain_terms[0],) = back(plan, 0, scalars, blocks, rows, grad, *setting)
    where = jnp.stack([place, core]).astype(jnp.int32)
    turned = turn(plan, where, mixed, [received[k] for k in range(1, depth)])
    turned, grads, gain_terms = lax.optimization_barrier((turned, grads, gain_terms))

    arrived = [grads[k] for k in range(1, depth)]
    theirs = term(plan, where, turned, last_grad, windows, arrived, True)
    mine = term(plan, where, turned, last_grad, windows, arrived, False)
    given = other_core(theirs)

    def piece(k):
        mine_k = lax.dynamic_index_in_dim(mine, chip ^ k, 0, keepdims=False).astype(F32)
        return mine_k + lax.dynamic_index_in_dim(given, chip ^ k, 0, keepdims=False).astype(F32)

    total = piece(0)
    for k in range(1, plan.chips):
        total = total + along_chips(piece(k).astype(BF16), k).astype(F32)

    terms = jnp.stack([gain_terms[s] for s in range(depth)])
    gain_sum = lax.dynamic_index_in_dim(terms, place, 0, keepdims=False)
    for k in range(1, depth):
        gain_sum = gain_sum + along_pipe(lax.dynamic_index_in_dim(terms, place ^ k, 0, keepdims=False), k)
    gain_sum = gain_sum + other_core(gain_sum)
    all_gains = [gain_sum] + [along_chips(gain_sum, k) for k in range(1, plan.chips)]
    all_gains = jnp.stack(all_gains)[chip ^ jnp.arange(plan.chips)]
    return (total[None], jnp.sum(all_gains, axis=0)[None, :2])


def solution(mesh):
    placed = (
        P(None, None, "dp", None),
        P(None, None, None, "dp"),
        P("pipe", "dp", None),
        P("pipe", None, None),
        P(None, None, "dp", None),
    )
    return jax.shard_map(
        shards,
        mesh=mesh,
        in_specs=placed,
        out_specs=(P("pipe", "dp", None), P("pipe", None, None)),
        check_vma=False,
    )
```

```python
import functools
import math

import jax
import jax.numpy as jnp
import numpy as np
from jax import lax
from jax.experimental import pallas as pl
from jax.experimental.pallas import tpu as pltpu
from jax.sharding import PartitionSpec as P

F32 = jnp.float32
BF16 = jnp.bfloat16
VMEM_BYTES = 56 * 1024 * 1024
CORES = 2
GAIN_ROWS = 8


def lane_tables(head):
    first = head // 8
    rest = (head - first) // 2
    coord = np.zeros(head, np.int32)
    freq = np.zeros(head, np.float32)
    sign = np.zeros(head, np.float32)
    partner = np.zeros(head, np.int32)
    offset = 0
    for axis, width in enumerate((first, rest, rest)):
        half = width // 2
        for j in range(half):
            low, high = offset + j, offset + j + half
            coord[low] = coord[high] = axis
            freq[low] = freq[high] = 256.0 ** (-2.0 * j / width)
            sign[low], sign[high] = -1.0, 1.0
            partner[low], partner[high] = high, low
        offset += width
    return coord, freq, sign, partner


def swap_lanes(x, partner):
    return jnp.take_along_axis(x, partner, axis=1, mode="promise_in_bounds")


def nt(a, b):
    return lax.dot_general(a, b, (((1,), (1,)), ((), ())), preferred_element_type=F32)


def tn(a, b):
    return lax.dot_general(a, b, (((0,), (0,)), ((), ())), preferred_element_type=F32)


def split(x):
    high = x.astype(BF16)
    return high, (x - high.astype(F32)).astype(BF16)


def fill_tables(tables, cos_ref, sin_ref, gain_ref, partner_ref, first=0):
    gain = gain_ref[...]
    turned = swap_lanes(gain, partner_ref[0 : gain.shape[0], :])
    factor = 1.0 / math.sqrt(gain.shape[-1])
    for t in range(tables.shape[0]):
        cosine, sine = cos_ref[first + t], sin_ref[first + t]
        tables[t, 0] = cosine * (gain[0:1] * factor)
        tables[t, 1] = sine * (turned[0:1] * factor)
        tables[t, 2] = cosine * gain[1:2]
        tables[t, 3] = sine * turned[1:2]


def project(hidden, mixed, weight, out, width):
    def part(i, carry):
        cols = pl.ds(pl.multiple_of(i * width, width), width)
        update = jnp.dot(mixed[...], weight[:, cols], preferred_element_type=F32)
        out[:, cols] = (hidden[:, cols].astype(F32) + update).astype(BF16)
        return carry

    lax.fori_loop(0, out.shape[1] // width, part, 0)


def pull_mixed(grad, weight, grad_mixed, width):
    def part(i, carry):
        cols = pl.ds(pl.multiple_of(i * width, width), width)
        grad_mixed[:, cols] = nt(grad[...], weight[cols, :]).astype(BF16)
        return carry

    lax.fori_loop(0, grad_mixed.shape[1] // width, part, 0)


def head_stage(pairs, hidden, tables, partner):
    values = [hidden[r, c] for _, r, c in pairs]
    wide = [v.astype(F32) for v in values]
    scale = [lax.rsqrt(jnp.mean(x * x, axis=-1, keepdims=True) + 1e-06) for x in wide]
    normed = [x * s for x, s in zip(wide, scale)]
    turned = [swap_lanes(n, partner) for n in normed]
    queries = [split(n * tables[t, 0] + w * tables[t, 1]) for (t, _, _), n, w in zip(pairs, normed, turned)]
    keys = [split(n * tables[t, 2] + w * tables[t, 3]) for (t, _, _), n, w in zip(pairs, normed, turned)]
    scores = [
        nt(jnp.concatenate([qh, ql, qh], axis=1), jnp.concatenate([kh, kh, kl], axis=1))
        for (qh, ql), (kh, kl) in zip(queries, keys)
    ]
    raised = [jnp.exp(s) for s in scores]
    weights = [e * (1.0 / jnp.sum(e, axis=-1, keepdims=True)) for e in raised]
    return values, normed, scale, [q[0] for q in queries], [k[0] for k in keys], weights


def head_pairs(step, groups, tok, head, together):
    cols = [pl.ds(pl.multiple_of((step * together + u) * head, head), head) for u in range(together)]
    return [(t, slice(t * tok, (t + 1) * tok), c) for c in cols for t in range(groups)]


def mix_rows(hidden, tables, partner_ref, mixed, tok, head, together):
    groups = hidden.shape[0] // tok
    partner = partner_ref[...]

    def some(i, carry):
        pairs = head_pairs(i, groups, tok, head, together)
        values, _, _, _, _, weights = head_stage(pairs, hidden, tables, partner)
        rounded = [w.astype(BF16) for w in weights]
        results = [jnp.dot(w, v, preferred_element_type=F32).astype(BF16) for w, v in zip(rounded, values)]
        for (_, r, c), m in zip(pairs, results):
            mixed[r, c] = m
        return carry

    lax.fori_loop(0, hidden.shape[1] // head // together, some, 0)


def pull_rows(
    hidden, grad, grad_mixed, tables, cos_ref, sin_ref, first, gain_ref, partner_ref, counts, sums, out, tok, head, together
):
    groups = hidden.shape[0] // tok
    partner = partner_ref[...]
    factor = 1.0 / math.sqrt(head)
    gain_q, gain_k = gain_ref[0:1, :] * factor, gain_ref[1:2, :]
    sums[...] = jnp.zeros(sums.shape, F32)

    def some(i, carry):
        pairs = head_pairs(i, groups, tok, head, together)
        values, normed, scale, queries, keys, weights = head_stage(pairs, hidden, tables, partner)
        above = [grad_mixed[r, c] for _, r, c in pairs]
        grad_weights = [nt(a, v).astype(BF16).astype(F32) for a, v in zip(above, values)]
        if out is not None:
            grad_values = [tn(w.astype(BF16), a) for w, a in zip(weights, above)]
        means = [jnp.sum(g * w, axis=-1, keepdims=True) for g, w in zip(grad_weights, weights)]
        grad_scores = [(w * (g - m)).astype(BF16) for w, g, m in zip(weights, grad_weights, means)]
        grad_q = [jnp.dot(s, k, preferred_element_type=F32) for s, k in zip(grad_scores, keys)]
        grad_k = [tn(s, q) for s, q in zip(grad_scores, queries)]
        swap_q = [swap_lanes(g, partner) for g in grad_q]
        swap_k = [swap_lanes(g, partner) for g in grad_k]
        back_q = [g * cos_ref[first + p[0]] - w * sin_ref[first + p[0]] for p, g, w in zip(pairs, grad_q, swap_q)]
        back_k = [g * cos_ref[first + p[0]] - w * sin_ref[first + p[0]] for p, g, w in zip(pairs, grad_k, swap_k)]
        for t in range(groups):
            mine = [j for j, p in enumerate(pairs) if p[0] == t]
            sums[t, 0] += sum(normed[j] * back_q[j] for j in mine)
            sums[t, 1] += sum(normed[j] * back_k[j] for j in mine)
        if out is not None:
            grad_normed = [q * gain_q + k * gain_k for q, k in zip(back_q, back_k)]
            along = [jnp.mean(n * g, axis=-1, keepdims=True) for n, g in zip(normed, grad_normed)]
            grad_hidden = [
                (v + s * (g - n * a)).astype(BF16).astype(F32)
                for v, s, g, n, a in zip(grad_values, scale, grad_normed, normed, along)
            ]
            for (_, r, c), g in zip(pairs, grad_hidden):
                out[r, c] = (grad[r, c].astype(F32) + g).astype(BF16)
        return carry

    lax.fori_loop(0, hidden.shape[1] // head // together, some, 0)
    total = [
        sum(counts[t] * jnp.sum(sums[t, i], axis=0, keepdims=True) for t in range(groups)) for i in range(2)
    ]
    return jnp.concatenate([total[0] * factor, total[1], jnp.zeros((GAIN_ROWS - 2, head), F32)], axis=0)


def params(flops, size):
    return dict(
        compiler_params=pltpu.CompilerParams(vmem_limit_bytes=VMEM_BYTES),
        cost_estimate=pl.CostEstimate(flops=flops, bytes_accessed=size, transcendentals=0),
    )


IN_VMEM = pl.BlockSpec(memory_space=pltpu.VMEM)
IN_SMEM = pl.BlockSpec(memory_space=pltpu.SMEM)
ANYWHERE = pl.BlockSpec(memory_space=pl.ANY)


class Plan:
    def parts_of(self, k):
        return 1 if k.bit_count() < 2 else self.depth.bit_length() - 1

    def __init__(self, clips, out_proj, qk_gains):
        self.depth = lax.axis_size("pipe")
        self.ways = lax.axis_size("dp")
        self.tok = clips.shape[2]
        self.channels = clips.shape[3]
        self.head = qk_gains.shape[-1]
        self.heads = self.channels // self.head
        self.tiles = clips.shape[0] * clips.shape[1]
        self.rows = out_proj.shape[1]
        self.share = self.tiles * self.tok // self.depth
        self.held = max(-(-(p * self.share % self.tok + self.share) // self.tok) for p in range(self.depth))
        self.span = self.held * self.tok
        self.width = math.gcd(self.channels, 512)
        self.chips = self.ways // CORES
        self.base_at = self.ways
        self.pieces = self.ways * sum(self.parts_of(k) for k in range(self.depth))
        self.window_at = self.base_at + 1
        self.place_at = self.base_at + 2
        self.counts_at = self.base_at + 3


def load_weight(plan, scalars, pieces, phase, buffer, sems):
    waits = []
    refs = iter(pieces)
    for i in range(plan.ways):
        first = scalars[i]
        for k in range(plan.depth):
            parts = plan.parts_of(k)
            size = plan.rows // parts
            copies = []
            for j in range(parts):
                rows = pl.ds(pl.multiple_of(first + j * size, math.gcd(size, 16)), size)
                copies.append(pltpu.make_async_copy(next(refs), buffer.at[rows], sems.at[i]))
            pl.when(scalars[plan.place_at] == phase ^ k)(functools.partial(start_all, copies))
        rows = buffer.at[pl.ds(pl.multiple_of(first, math.gcd(plan.rows, 16)), plan.rows)]
        waits.append(pltpu.make_async_copy(rows, rows, sems.at[i]))
    return waits


def start_all(copies):
    for copy in copies:
        copy.start()


def wait_all(copies):
    for copy in copies:
        copy.wait()


def window_of(plan, scalars):
    return pl.ds(pl.multiple_of(scalars[plan.window_at], math.gcd(plan.share, plan.tok)), plan.share)


def own_rows(plan, scalars):
    return pl.ds(pl.multiple_of(scalars[plan.base_at] * plan.tok, plan.tok), plan.span)


def forward_kernel(scalars, *refs, plan):
    stacks, refs = refs[: plan.pieces], refs[plan.pieces :]
    rows, cos_ref, sin_ref, gains, partner_ref = refs[:5]
    states_out, sent_out, refs = refs[5], refs[6 : 6 + plan.depth], refs[6 + plan.depth :]
    buffer, start, states, sent, mixed, tables, sems, row_sem, state_sems, sent_sems = refs
    last = plan.depth - 1
    base = scalars[plan.base_at]
    load = pltpu.make_async_copy(rows.at[own_rows(plan, scalars)], start, row_sem.at[0])
    load.start()

    def fetch(phase):
        return load_weight(plan, scalars, stacks, phase, buffer.at[phase % 2], sems.at[phase % 2])

    coming = {phase: fetch(phase) for phase in range(min(2, last))}
    going = []
    for phase in range(plan.depth):
        hidden = states.at[phase - 1] if phase else start
        fill_tables(tables, cos_ref, sin_ref, gains.at[scalars[plan.place_at] ^ phase], partner_ref, base)
        if phase == 0:
            load.wait()
        mix_rows(hidden, tables, partner_ref, mixed, plan.tok, plan.head, plan.heads)
        sent[phase] = mixed[window_of(plan, scalars), :]
        going.append(pltpu.make_async_copy(sent.at[phase], sent_out[phase], sent_sems.at[phase]))
        going[-1].start()
        if phase < last:
            wait_all(coming[phase])
            project(hidden, mixed, buffer.at[phase % 2], states.at[phase], plan.width)
            going.append(pltpu.make_async_copy(states.at[phase], states_out.at[phase], state_sems.at[phase]))
            going[-1].start()
            if phase + 2 < last:
                coming[phase + 2] = fetch(phase + 2)
    wait_all(going)


def forward(plan, scalars, stacks, rows, cos, sin, gains, partner):
    shape = jax.ShapeDtypeStruct
    states = (plan.depth - 1, plan.span, plan.channels)
    return pl.pallas_call(
        functools.partial(forward_kernel, plan=plan),
        out_shape=(shape(states, BF16), *[shape((plan.share, plan.channels), BF16)] * plan.depth),
        in_specs=[IN_SMEM] + [ANYWHERE] * (len(stacks) + 1) + [IN_VMEM] * 4,
        out_specs=(ANYWHERE,) * (plan.depth + 1),
        scratch_shapes=[
            pltpu.VMEM((2, plan.channels, plan.channels), BF16),
            pltpu.VMEM((plan.span, plan.channels), BF16),
            pltpu.VMEM(states, BF16),
            pltpu.VMEM((plan.depth, plan.share, plan.channels), BF16),
            pltpu.VMEM((plan.span, plan.channels), BF16),
            pltpu.VMEM((plan.held, 4, plan.tok, plan.head), F32),
            pltpu.SemaphoreType.DMA((2, plan.ways)),
            pltpu.SemaphoreType.DMA((1,)),
            pltpu.SemaphoreType.DMA((plan.depth - 1,)),
            pltpu.SemaphoreType.DMA((plan.depth,)),
        ],
        name="forward",
        **params(2 * plan.depth * plan.span * plan.channels * plan.channels, 2 * plan.depth * plan.channels**2),
    )(scalars, *stacks, rows, cos, sin, gains, partner)


def back_kernel(scalars, *refs, plan, phases):
    stacks, refs = refs[: plan.pieces], refs[plan.pieces :]
    states, grad_any, cos_ref, sin_ref, gains, partner_ref = refs[:6]
    top, count = phases[0], len(phases)
    grad_out, gain_out, sent_out, refs = refs[6], refs[7], refs[8 : 8 + count], refs[8 + count :]
    buffer, hidden, sent, grad_mixed, tables, sums, sems, state_sems, row_sem, sent_sems = refs
    base = scalars[plan.base_at]
    counts = [scalars[plan.counts_at + t].astype(F32) for t in range(plan.held)]
    source = grad_any.at[own_rows(plan, scalars)] if top == plan.depth - 1 else grad_any
    load = pltpu.make_async_copy(source, grad_out, row_sem.at[0])
    load.start()

    def fetch(phase):
        slot = phase % 2
        waits = load_weight(plan, scalars, stacks, phase, buffer.at[slot], sems.at[slot])
        waits.append(pltpu.make_async_copy(states.at[phase - 1], hidden.at[slot], state_sems.at[slot]))
        waits[-1].start()
        return waits

    coming = {phase: fetch(phase) for phase in phases[:2]}
    load.wait()
    going = []
    for i, phase in enumerate(phases):
        slot = phase % 2
        fill_tables(tables, cos_ref, sin_ref, gains.at[scalars[plan.place_at] ^ phase], partner_ref, base)
        wait_all(coming[phase])
        pull_mixed(grad_out, buffer.at[slot], grad_mixed, plan.width)
        gain_out[i] = pull_rows(
            hidden.at[slot], grad_out, grad_mixed, tables, cos_ref, sin_ref, base, gains.at[scalars[plan.place_at] ^ phase], partner_ref, counts,
            sums, grad_out, plan.tok, plan.head, plan.heads,
        )
        sent[i] = grad_out[window_of(plan, scalars), :]
        going.append(pltpu.make_async_copy(sent.at[i], sent_out[i], sent_sems.at[i]))
        going[-1].start()
        if phase - 2 in phases:
            coming[phase - 2] = fetch(phase - 2)
    wait_all(going)


def back(plan, phases, scalars, stacks, states, grad, cos, sin, gains, partner):
    shape = jax.ShapeDtypeStruct
    count = len(phases)
    return pl.pallas_call(
        functools.partial(back_kernel, plan=plan, phases=phases),
        out_shape=(
            shape((plan.span, plan.channels), BF16),
            shape((count, GAIN_ROWS, plan.head), F32),
            *[shape((plan.share, plan.channels), BF16)] * count,
        ),
        in_specs=[IN_SMEM] + [ANYWHERE] * (len(stacks) + 2) + [IN_VMEM] * 4,
        out_specs=(IN_VMEM, IN_VMEM, *[ANYWHERE] * count),
        scratch_shapes=[
            pltpu.VMEM((2, plan.channels, plan.channels), BF16),
            pltpu.VMEM((2, plan.span, plan.channels), BF16),
            pltpu.VMEM((count, plan.share, plan.channels), BF16),
            pltpu.VMEM((plan.span, plan.channels), BF16),
            pltpu.VMEM((plan.held, 4, plan.tok, plan.head), F32),
            pltpu.VMEM((plan.held, 2, plan.tok, plan.head), F32),
            pltpu.SemaphoreType.DMA((2, plan.ways)),
            pltpu.SemaphoreType.DMA((2,)),
            pltpu.SemaphoreType.DMA((1,)),
            pltpu.SemaphoreType.DMA((count,)),
        ],
        name="back",
        **params(6 * count * plan.span * plan.channels * plan.channels, 3 * count * plan.channels**2),
    )(scalars, *stacks, states, grad, cos, sin, gains, partner)


def first_back_kernel(scalars, *refs, plan):
    stacks, refs = refs[: plan.pieces], refs[plan.pieces :]
    rows, grad_any, cos_ref, sin_ref, gains, partner_ref, gain_out = refs[:7]
    buffer, hidden, grad_in, grad_mixed, tables, sums, sems, row_sems = refs[7:]
    base = scalars[plan.base_at]
    counts = [scalars[plan.counts_at + t].astype(F32) for t in range(plan.held)]
    copies = [
        pltpu.make_async_copy(grad_any, grad_in, row_sems.at[0]),
        pltpu.make_async_copy(rows.at[own_rows(plan, scalars)], hidden, row_sems.at[1]),
    ]
    start_all(copies)
    copies += load_weight(plan, scalars, stacks, 0, buffer, sems)
    fill_tables(tables, cos_ref, sin_ref, gains.at[scalars[plan.place_at]], partner_ref, base)
    wait_all(copies)
    pull_mixed(grad_in, buffer, grad_mixed, plan.width)
    gain_out[...] = pull_rows(
        hidden, grad_in, grad_mixed, tables, cos_ref, sin_ref, base, gains.at[scalars[plan.place_at]], partner_ref, counts, sums, None,
        plan.tok, plan.head, plan.heads,
    )


def first_back(plan, scalars, stacks, rows, grad_in, cos, sin, gains, partner):
    held = pltpu.VMEM((plan.span, plan.channels), BF16)
    return pl.pallas_call(
        functools.partial(first_back_kernel, plan=plan),
        out_shape=jax.ShapeDtypeStruct((GAIN_ROWS, plan.head), F32),
        in_specs=[IN_SMEM] + [ANYWHERE] * (len(stacks) + 2) + [IN_VMEM] * 4,
        out_specs=IN_VMEM,
        scratch_shapes=[
            pltpu.VMEM((plan.channels, plan.channels), BF16),
            held,
            held,
            held,
            pltpu.VMEM((plan.held, 4, plan.tok, plan.head), F32),
            pltpu.VMEM((plan.held, 2, plan.tok, plan.head), F32),
            pltpu.SemaphoreType.DMA((plan.ways,)),
            pltpu.SemaphoreType.DMA((2,)),
        ],
        name="first_back",
        **params(6 * plan.span * plan.channels * plan.channels, 3 * plan.channels**2),
    )(scalars, *stacks, rows, grad_in, cos, sin, gains, partner)


def turn_kernel(place, *refs, plan):
    count = 2 * plan.depth - 1
    sets = [refs[:count], refs[count : 2 * count]]
    out, gathered, turned, sems = refs[2 * count :]
    copies = []
    for half, (own, received) in enumerate((x[: plan.depth], x[plan.depth :]) for x in sets):
        for k in range(plan.depth):
            at = half * plan.depth + k
            rows = gathered.at[pl.ds(at * plan.share, plan.share)]
            if k:
                copies.append(pltpu.make_async_copy(received[k - 1], rows, sems.at[at]))
                copies[-1].start()
            else:
                for phase in range(plan.depth):
                    copy = pltpu.make_async_copy(own[phase], rows, sems.at[at])
                    pl.when(place[0] == phase)(copy.start)
                copies.append(copy)
    wait_all(copies)

    def part(i, carry):
        cols = pl.ds(pl.multiple_of(i * plan.width, plan.width), plan.width)
        turned[cols, :] = gathered[:, cols].T
        return carry

    lax.fori_loop(0, plan.channels // plan.width, part, 0)
    for k in range(plan.chips):
        start = ((place[2] ^ k) * CORES + place[1]) * plan.rows
        out[k] = turned[pl.ds(pl.multiple_of(start, math.gcd(plan.rows, 16)), plan.rows), :]


def turn(plan, place, own, received, own_other, received_other):
    total = 2 * plan.depth * plan.share
    return pl.pallas_call(
        functools.partial(turn_kernel, plan=plan),
        out_shape=jax.ShapeDtypeStruct((plan.chips, plan.rows, total), BF16),
        in_specs=[IN_SMEM] + [ANYWHERE] * (4 * plan.depth - 2),
        out_specs=IN_VMEM,
        scratch_shapes=[
            pltpu.VMEM((total, plan.channels), BF16),
            pltpu.VMEM((plan.channels, total), BF16),
            pltpu.SemaphoreType.DMA((2 * plan.depth,)),
        ],
        name="turn",
        **params(0, 4 * total * plan.channels),
    )(place, *own, *received, *own_other, *received_other)


def term_kernel(place, turned_any, cot, cot_other, *refs, plan):
    count = 2 * plan.depth - 2
    sets, refs = [refs[:count], refs[count : 2 * count]], refs[2 * count :]
    outs, (turned, grads, terms, sems, turned_sem, out_sems) = refs[: plan.chips], refs[plan.chips :]
    total = 2 * plan.depth
    chunks = [pl.ds(i * plan.width, plan.width) for i in range(plan.channels // plan.width)]
    load = pltpu.make_async_copy(turned_any, turned, turned_sem.at[0])
    load.start()

    def gather(phase):
        for i, cols in enumerate(chunks):
            for at in range(total):
                half, k = divmod(at, plan.depth)
                if phase == plan.depth - 1:
                    source = (cot, cot_other)[half].at[pl.ds((phase ^ k) * plan.share, plan.share), cols]
                else:
                    source = (sets[half][plan.depth - 2 + k] if k else sets[half][phase]).at[:, cols]
                target = grads.at[i, pl.ds(at * plan.share, plan.share)]
                pltpu.make_async_copy(source, target, sems.at[i, at]).start()

    for phase in range(plan.depth):
        pl.when(place[0] == phase)(functools.partial(gather, phase))
    load.wait()
    going = []
    for i, cols in enumerate(chunks):
        for at in range(total):
            rows = grads.at[i, pl.ds(at * plan.share, plan.share)]
            pltpu.make_async_copy(rows, rows, sems.at[i, at]).wait()
        for k in range(plan.chips):
            terms[i, k] = jnp.dot(turned[k], grads[i], preferred_element_type=F32).astype(BF16)
            going.append(pltpu.make_async_copy(terms.at[i, k], outs[k].at[:, cols], out_sems.at[i, k]))
            going[-1].start()
    wait_all(going)


def term(plan, place, turned, cot, cot_other, windows, received, windows_other, received_other):
    total = 2 * plan.depth * plan.share
    chunks = plan.channels // plan.width
    given = [*windows, *received, *windows_other, *received_other]
    return pl.pallas_call(
        functools.partial(term_kernel, plan=plan),
        out_shape=[jax.ShapeDtypeStruct((plan.rows, plan.channels), BF16)] * plan.chips,
        in_specs=[IN_SMEM] + [ANYWHERE] * (3 + len(given)),
        out_specs=[ANYWHERE] * plan.chips,
        scratch_shapes=[
            pltpu.VMEM((plan.chips, plan.rows, total), BF16),
            pltpu.VMEM((chunks, total, plan.width), BF16),
            pltpu.VMEM((chunks, plan.chips, plan.rows, plan.width), BF16),
            pltpu.SemaphoreType.DMA((chunks, 2 * plan.depth)),
            pltpu.SemaphoreType.DMA((1,)),
            pltpu.SemaphoreType.DMA((chunks, plan.chips)),
        ],
        name="term",
        **params(total * plan.channels**2, 4 * plan.channels**2),
    )(place, turned, cot, cot_other, *given)


def along_pipe(x, k):
    return lax.ppermute(x, "pipe", [(i, i ^ k) for i in range(lax.axis_size("pipe"))])


def along_chips(x, k):
    return lax.ppermute(x, "dp", [(i, i ^ (CORES * k)) for i in range(lax.axis_size("dp"))])


def other_core(x):
    return lax.ppermute(x, "dp", [(i, i ^ 1) for i in range(lax.axis_size("dp"))])


def spread_near(block, depth):
    return {1 << bit: along_pipe(block, 1 << bit) for bit in range(depth.bit_length() - 1)}


def spread_far(near, depth):
    bits = depth.bit_length() - 1
    part = near[1].shape[0] // bits
    got = {k: [x[i * part : (i + 1) * part] for i in range(bits)] for k, x in near.items()}
    for k in sorted(range(1, depth), key=lambda k: k.bit_count()):
        if k not in got:
            got[k] = []
            for i in range(bits):
                order = [(i + b) % bits for b in range(bits)]
                bit = 1 << [b for b in order if k >> b & 1][-1]
                got[k].append(along_pipe(got[k ^ bit][i], bit))
    return {k: parts for k, parts in got.items() if k not in near}


def gather_weights(plan, own, gain, chip, beside):
    chips, depth = plan.chips, plan.depth
    order = [sorted((b for b in range(chips) if b != c), key=lambda b: (abs(b - c), b ^ c)) for c in range(chips)]
    up = down = block = own
    arrived = {}
    ours, nears, theirs, gains, extra = [], [], [], (), ()

    def swapped(i, keys):
        return {k: [other_core(x) for x in ours[i][k]] for k in keys}

    near_keys = [k for k in range(depth) if k.bit_count() < 2]
    far_keys = [k for k in range(depth) if k.bit_count() > 1]

    for step in range(1, chips + 1):
        near = spread_near(block, depth)
        if step == 1:
            gains = [along_pipe(gain, k) for k in range(1, depth)]
        if step == 2:
            extra = beside(jnp.asarray([[c, *order[c]] for c in range(chips)], jnp.int32)[chip])
        far = spread_far(nears[-1], depth) if step > 1 else {}
        swaps = []
        if step > 2:
            swaps = [swapped(step - 3, range(depth))]
        if step < chips:
            up = lax.ppermute(up, "dp", [(i, i + CORES) for i in range(plan.ways - CORES)])
            down = lax.ppermute(down, "dp", [(i + CORES, i) for i in range(plan.ways - CORES)])
        up, down, near, gains, extra, swaps = lax.optimization_barrier(
            (up, down, near, gains, extra, swaps)
        )
        theirs += swaps
        if step > 1:
            ours[-1].update(far)
        nears.append(near)
        ours.append({0: [block], **{k: [x] for k, x in near.items()}})
        arrived[step, -1], arrived[step, 1] = up, down
        if step < chips:
            places = {}
            for c in range(chips):
                b = order[c][step - 1]
                places.setdefault((abs(b - c), 1 if b > c else -1), []).append(c)
            (first, _), *rest = places.items()
            block = arrived[first]
            for key, members in rest:
                here = functools.reduce(jnp.logical_or, [chip == c for c in members])
                block = jnp.where(here, arrived[key], block)
    far = spread_far(nears[-1], depth)
    left = [swapped(i, range(depth)) for i in range(len(theirs), chips - 1)] + [swapped(chips - 1, near_keys)]
    ours[-1].update(far)
    theirs += left
    theirs[-1].update(swapped(chips - 1, far_keys))
    pieces = [x for block in ours + theirs for k in range(depth) for x in block[k]]
    return pieces, jnp.stack([gain, *gains]).astype(F32), extra


def shards(clips, positions, out_proj, qk_gains, cotangent):
    plan = Plan(clips, out_proj, qk_gains)
    depth, last = plan.depth, plan.depth - 1
    place = lax.axis_index("pipe")
    member = lax.axis_index("dp")
    chip, core = member // CORES, member % CORES
    rows = clips.reshape(plan.tiles * plan.tok, plan.channels)
    last_grad = cotangent.reshape(plan.tiles * plan.tok, plan.channels)
    coord, freq, sign, partner = lane_tables(plan.head)
    own_gain = jnp.pad(qk_gains[0], ((0, GAIN_ROWS - 2), (0, 0)))
    first_row = place * plan.share
    base = jnp.minimum(first_row // plan.tok, plan.tiles - plan.held)
    tile_starts = (base + jnp.arange(plan.held)) * plan.tok
    counts = ((tile_starts >= first_row) & (tile_starts < first_row + plan.share)).astype(jnp.int32)

    def settings(whose):
        spots = positions.reshape(3, plan.tiles, plan.tok, 1).astype(F32)
        angle = jnp.where(coord == 0, spots[0], jnp.where(coord == 1, spots[1], spots[2])) * freq
        partners = jnp.broadcast_to(jnp.asarray(partner), (plan.tok, plan.head))
        starts = [(whose * CORES + core) * plan.rows, (whose * CORES + 1 - core) * plan.rows]
        more = jnp.stack([base, first_row - base * plan.tok, place])
        scalars = jnp.concatenate([*starts, more, counts]).astype(jnp.int32)
        return scalars, jnp.cos(angle), jnp.sin(angle) * sign, partners

    blocks, gains, (scalars, cos, sin, partners) = gather_weights(plan, out_proj[0], own_gain, chip, settings)
    setting = (cos, sin, gains, partners)

    def to_owners(windows):
        got = []
        for k in range(1, depth):
            chosen = windows[0]
            for phase in range(1, len(windows)):
                chosen = jnp.where(place ^ k == phase, windows[phase], chosen)
            got.append(lax.ppermute(chosen, "pipe", [(i, i ^ k) for i in range(depth) if i ^ k < len(windows)]))
        return got

    states, *mixed = forward(plan, scalars, blocks, rows, *setting)
    received = to_owners(mixed)
    near = [k - 1 for k in range(1, depth) if k.bit_count() == 1]
    far = [k - 1 for k in range(1, depth) if k.bit_count() > 1]
    grad, terms, windows = last_grad, [], []
    upper = range(last, 1, -1)
    if upper:
        grad, gain, *windows = back(plan, upper, scalars, blocks, states, grad, *setting)
        terms.append(gain)
    mixed_other, cot_other = [other_core(x) for x in mixed], other_core(last_grad)
    grad, arrived, mixed_other, cot_other = lax.optimization_barrier(
        (grad, [received[i] for i in near], mixed_other, cot_other)
    )
    for i, x in zip(near, arrived):
        received[i] = x
    received_other = {i: other_core(received[i]) for i in near}
    windows_other = [other_core(x) for x in windows]
    grad, gain, window = back(plan, range(1, 0, -1), scalars, blocks, states, grad, *setting)
    grad, window, arrived, received_other, windows_other = lax.optimization_barrier(
        (grad, window, [received[i] for i in far], received_other, windows_other)
    )
    for i, x in zip(far, arrived):
        received[i] = x
    windows = [window, *reversed(windows)]
    terms = jnp.concatenate([*terms, gain], axis=0)[::-1]
    grads = to_owners(windows)
    first_term = first_back(plan, scalars, blocks, rows, grad, *setting)
    where = jnp.stack([place, core, chip]).astype(jnp.int32)
    received_other.update({i: other_core(received[i]) for i in far})
    windows_other = [other_core(window), *reversed(windows_other)]
    turned = turn(plan, where, mixed, received, mixed_other, [received_other[i] for i in range(last)])
    turned, windows_other, first_term, arrived = lax.optimization_barrier(
        (turned, windows_other, first_term, [grads[i] for i in far])
    )
    for i, x in zip(far, arrived):
        grads[i] = x

    grads_other = [other_core(x) for x in grads]
    pieces = term(plan, where, turned, last_grad, cot_other, windows, grads, windows_other, grads_other)
    total = pieces[0].astype(F32)
    for k in range(1, plan.chips):
        total = total + along_chips(pieces[k], k).astype(F32)

    terms = jnp.concatenate([first_term[None], terms], axis=0)
    gain_sum = lax.dynamic_index_in_dim(terms, place, 0, keepdims=False)
    for k in range(1, depth):
        gain_sum = gain_sum + along_pipe(lax.dynamic_index_in_dim(terms, place ^ k, 0, keepdims=False), k)
    gain_sum = gain_sum + other_core(gain_sum)
    all_gains = [gain_sum] + [along_chips(gain_sum, k) for k in range(1, plan.chips)]
    all_gains = jnp.stack(all_gains)[chip ^ jnp.arange(plan.chips)]
    return (total[None], jnp.sum(all_gains, axis=0)[None, :2])


def solution(mesh):
    placed = (
        P(None, None, "dp", None),
        P(None, None, None, "dp"),
        P("pipe", "dp", None),
        P("pipe", None, None),
        P(None, None, "dp", None),
    )
    return jax.shard_map(
        shards,
        mesh=mesh,
        in_specs=placed,
        out_specs=(P("pipe", "dp", None), P("pipe", None, None)),
        check_vma=False,
    )
```

```python
import functools
import math

import jax
import jax.numpy as jnp
import numpy as np
from jax import lax
from jax.experimental import pallas as pl
from jax.experimental.pallas import tpu as pltpu
from jax.sharding import PartitionSpec as P

F32 = jnp.float32
BF16 = jnp.bfloat16
VMEM_BYTES = 56 * 1024 * 1024
CORES = 2
GAIN_ROWS = 8
GAIN_PARTS = 3
EXTRA_ROWS = 16


def lane_tables(head):
    first = head // 8
    rest = (head - first) // 2
    coord = np.zeros(head, np.int32)
    freq = np.zeros(head, np.float32)
    sign = np.zeros(head, np.float32)
    partner = np.zeros(head, np.int32)
    offset = 0
    for axis, width in enumerate((first, rest, rest)):
        half = width // 2
        for j in range(half):
            low, high = offset + j, offset + j + half
            coord[low] = coord[high] = axis
            freq[low] = freq[high] = 256.0 ** (-2.0 * j / width)
            sign[low], sign[high] = -1.0, 1.0
            partner[low], partner[high] = high, low
        offset += width
    return coord, freq, sign, partner


def nt(a, b):
    return lax.dot_general(a, b, (((1,), (1,)), ((), ())), preferred_element_type=F32)


def tn(a, b):
    return lax.dot_general(a, b, (((0,), (0,)), ((), ())), preferred_element_type=F32)


def split(x):
    high = x.astype(BF16)
    return high, (x - high.astype(F32)).astype(BF16)


def fill_tables(tables, cos_ref, sin_ref, gain_ref, swap_ref, first=0):
    gain = gain_ref[...]
    turned = jnp.dot(gain.astype(BF16), swap_ref[...], preferred_element_type=F32)
    factor = 1.0 / math.sqrt(gain.shape[-1])
    query, query_turned, key, key_turned = gain[0:1] * factor, turned[0:1] * factor, gain[1:2], turned[1:2]
    for t in range(tables.shape[0]):
        cosine, sine = cos_ref[first + t], sin_ref[first + t]
        tables[t, 0] = cosine * query
        tables[t, 1] = sine * query_turned
        tables[t, 2] = cosine * key
        tables[t, 3] = sine * key_turned
        if tables.shape[1] > 4:
            tables[t, 4] = cosine * query_turned
            tables[t, 5] = -sine * query
            tables[t, 6] = cosine * key_turned
            tables[t, 7] = -sine * key


def project(hidden, mixed, weight, out, width):
    def part(i, carry):
        cols = pl.ds(pl.multiple_of(i * width, width), width)
        update = jnp.dot(mixed[...], weight[:, cols], preferred_element_type=F32)
        out[:, cols] = (hidden[:, cols].astype(F32) + update).astype(BF16)
        return carry

    lax.fori_loop(0, out.shape[1] // width, part, 0)


def pull_mixed(grad, weight, grad_mixed, width):
    def part(i, carry):
        cols = pl.ds(pl.multiple_of(i * width, width), width)
        grad_mixed[:, cols] = nt(grad[...], weight[cols, :]).astype(BF16)
        return carry

    lax.fori_loop(0, grad_mixed.shape[1] // width, part, 0)


def head_stage(pairs, hidden, tables, swap):
    values = [hidden[r, c] for _, r, c in pairs]
    wide = [v.astype(F32) for v in values]
    scale = [lax.rsqrt(jnp.mean(x * x, axis=-1, keepdims=True) + 1e-06) for x in wide]
    turned = [jnp.dot(v, swap, preferred_element_type=F32) * s for v, s in zip(values, scale)]
    normed = [x * s for x, s in zip(wide, scale)]
    queries = [split(n * tables[t, 0] + w * tables[t, 1]) for (t, _, _), n, w in zip(pairs, normed, turned)]
    keys = [split(n * tables[t, 2] + w * tables[t, 3]) for (t, _, _), n, w in zip(pairs, normed, turned)]
    scores = [
        nt(jnp.concatenate([qh, ql, qh], axis=1), jnp.concatenate([kh, kh, kl], axis=1))
        for (qh, ql), (kh, kl) in zip(queries, keys)
    ]
    raised = [jnp.exp(s) for s in scores]
    weights = [e * (1.0 / jnp.sum(e, axis=-1, keepdims=True)) for e in raised]
    return values, normed, turned, scale, [q[0] for q in queries], [k[0] for k in keys], weights


def head_pairs(step, groups, tok, head, together):
    cols = [pl.ds(pl.multiple_of((step * together + u) * head, head), head) for u in range(together)]
    return [(t, slice(t * tok, (t + 1) * tok), c) for c in cols for t in range(groups)]


def mix_rows(hidden, tables, swap_ref, mixed, tok, head, together):
    groups = hidden.shape[0] // tok
    swap = swap_ref[...]

    def some(i, carry):
        pairs = head_pairs(i, groups, tok, head, together)
        values, _, _, _, _, _, weights = head_stage(pairs, hidden, tables, swap)
        rounded = [w.astype(BF16) for w in weights]
        results = [jnp.dot(w, v, preferred_element_type=F32).astype(BF16) for w, v in zip(rounded, values)]
        for (_, r, c), m in zip(pairs, results):
            mixed[r, c] = m
        return carry

    lax.fori_loop(0, hidden.shape[1] // head // together, some, 0)


def pull_rows(
    hidden, grad, grad_mixed, tables, cos_ref, sin_ref, first, gain_ref, swap_ref, counts, sums, out, tok, head, together
):
    groups = hidden.shape[0] // tok
    swap = swap_ref[...]
    factor = 1.0 / math.sqrt(head)
    gain_q, gain_k = gain_ref[0:1, :] * factor, gain_ref[1:2, :]
    sums[...] = jnp.zeros(sums.shape, F32)

    def some(i, carry):
        pairs = head_pairs(i, groups, tok, head, together)
        values, normed, turned, scale, queries, keys, weights = head_stage(pairs, hidden, tables, swap)
        queries = [
            jnp.concatenate([q, (w * tables[t, 4] + n * tables[t, 5]).astype(BF16)], axis=1)
            for (t, _, _), q, n, w in zip(pairs, queries, normed, turned)
        ]
        keys = [
            jnp.concatenate([k, (w * tables[t, 6] + n * tables[t, 7]).astype(BF16)], axis=1)
            for (t, _, _), k, n, w in zip(pairs, keys, normed, turned)
        ]
        above = [grad_mixed[r, c] for _, r, c in pairs]
        grad_weights = [nt(a, v).astype(BF16).astype(F32) for a, v in zip(above, values)]
        if out is not None:
            grad_values = [tn(w.astype(BF16), a) for w, a in zip(weights, above)]
        means = [jnp.sum(g * w, axis=-1, keepdims=True) for g, w in zip(grad_weights, weights)]
        grad_scores = [(w * (g - m)).astype(BF16) for w, g, m in zip(weights, grad_weights, means)]
        grad_q = [jnp.dot(s, k, preferred_element_type=F32) for s, k in zip(grad_scores, keys)]
        grad_k = [tn(s, q) for s, q in zip(grad_scores, queries)]
        back_q = [g[:, :head] * cos_ref[first + p[0]] - g[:, head:] * sin_ref[first + p[0]] for p, g in zip(pairs, grad_q)]
        back_k = [g[:, :head] * cos_ref[first + p[0]] - g[:, head:] * sin_ref[first + p[0]] for p, g in zip(pairs, grad_k)]
        for t in range(groups):
            mine = [j for j, p in enumerate(pairs) if p[0] == t]
            sums[t, 0] += sum(normed[j] * back_q[j] for j in mine)
            sums[t, 1] += sum(normed[j] * back_k[j] for j in mine)
        if out is not None:
            grad_normed = [q * gain_q + k * gain_k for q, k in zip(back_q, back_k)]
            along = [jnp.mean(n * g, axis=-1, keepdims=True) for n, g in zip(normed, grad_normed)]
            grad_hidden = [
                (v + s * (g - n * a)).astype(BF16).astype(F32)
                for v, s, g, n, a in zip(grad_values, scale, grad_normed, normed, along)
            ]
            for (_, r, c), g in zip(pairs, grad_hidden):
                out[r, c] = (grad[r, c].astype(F32) + g).astype(BF16)
        return carry

    lax.fori_loop(0, hidden.shape[1] // head // together, some, 0)
    total = [
        sum(counts[t] * jnp.sum(sums[t, i], axis=0, keepdims=True) for t in range(groups)) for i in range(2)
    ]
    return jnp.concatenate([total[0] * factor, total[1], jnp.zeros((GAIN_ROWS - 2, head), F32)], axis=0)


def params(flops, size):
    return dict(
        compiler_params=pltpu.CompilerParams(vmem_limit_bytes=VMEM_BYTES),
        cost_estimate=pl.CostEstimate(flops=flops, bytes_accessed=size, transcendentals=0),
    )


IN_VMEM = pl.BlockSpec(memory_space=pltpu.VMEM)
IN_SMEM = pl.BlockSpec(memory_space=pltpu.SMEM)
ANYWHERE = pl.BlockSpec(memory_space=pl.ANY)


class Plan:
    def parts_of(self, k):
        return 1 if k.bit_count() < 2 else self.depth.bit_length() - 1

    def __init__(self, clips, out_proj, qk_gains):
        self.depth = lax.axis_size("pipe")
        self.ways = lax.axis_size("dp")
        self.tok = clips.shape[2]
        self.channels = clips.shape[3]
        self.head = qk_gains.shape[-1]
        self.heads = self.channels // self.head
        self.tiles = clips.shape[0] * clips.shape[1]
        self.rows = out_proj.shape[1]
        self.share = self.tiles * self.tok // self.depth
        self.held = max(-(-(p * self.share % self.tok + self.share) // self.tok) for p in range(self.depth))
        self.span = self.held * self.tok
        self.width = math.gcd(self.channels, 512)
        self.chips = self.ways // CORES
        self.base_at = self.ways
        self.pieces = self.ways * sum(self.parts_of(k) for k in range(self.depth))
        self.window_at = self.base_at + 1
        self.place_at = self.base_at + 2
        self.counts_at = self.base_at + 3


def load_weight(plan, scalars, pieces, phase, buffer, sems):
    waits = []
    refs = iter(pieces)
    for i in range(plan.ways):
        first = scalars[i]
        for k in range(plan.depth):
            parts = plan.parts_of(k)
            size = plan.rows // parts
            copies = []
            for j in range(parts):
                rows = pl.ds(pl.multiple_of(first + j * size, math.gcd(size, 16)), size)
                copies.append(pltpu.make_async_copy(next(refs), buffer.at[rows], sems.at[i]))
            pl.when(scalars[plan.place_at] == phase ^ k)(functools.partial(start_all, copies))
        rows = buffer.at[pl.ds(pl.multiple_of(first, math.gcd(plan.rows, 16)), plan.rows)]
        waits.append(pltpu.make_async_copy(rows, rows, sems.at[i]))
    return waits


def start_all(copies):
    for copy in copies:
        copy.start()


def wait_all(copies):
    for copy in copies:
        copy.wait()


def window_of(plan, scalars):
    return pl.ds(pl.multiple_of(scalars[plan.window_at], math.gcd(plan.share, plan.tok)), plan.share)


def own_rows(plan, scalars):
    return pl.ds(pl.multiple_of(scalars[plan.base_at] * plan.tok, plan.tok), plan.span)


def forward_kernel(scalars, *refs, plan):
    stacks, refs = refs[: plan.pieces], refs[plan.pieces :]
    rows, cos_ref, sin_ref, gains, swap_ref = refs[:5]
    states_out, sent_out, refs = refs[5], refs[6 : 6 + plan.depth], refs[6 + plan.depth :]
    buffer, start, states, sent, mixed, tables, sems, row_sem, state_sems, sent_sems = refs
    last = plan.depth - 1
    base = scalars[plan.base_at]
    load = pltpu.make_async_copy(rows.at[own_rows(plan, scalars)], start, row_sem.at[0])
    load.start()

    def fetch(phase):
        return load_weight(plan, scalars, stacks, phase, buffer.at[phase % 2], sems.at[phase % 2])

    coming = {phase: fetch(phase) for phase in range(min(2, last))}
    going = []
    for phase in range(plan.depth):
        hidden = states.at[phase - 1] if phase else start
        fill_tables(tables, cos_ref, sin_ref, gains.at[scalars[plan.place_at] ^ phase], swap_ref, base)
        if phase == 0:
            load.wait()
        mix_rows(hidden, tables, swap_ref, mixed, plan.tok, plan.head, plan.heads)
        sent[phase] = mixed[window_of(plan, scalars), :]
        going.append(pltpu.make_async_copy(sent.at[phase], sent_out[phase], sent_sems.at[phase]))
        going[-1].start()
        if phase < last:
            wait_all(coming[phase])
            project(hidden, mixed, buffer.at[phase % 2], states.at[phase], plan.width)
            going.append(pltpu.make_async_copy(states.at[phase], states_out.at[phase], state_sems.at[phase]))
            going[-1].start()
            if phase + 2 < last:
                coming[phase + 2] = fetch(phase + 2)
    wait_all(going)


def forward(plan, scalars, stacks, rows, cos, sin, gains, swap):
    shape = jax.ShapeDtypeStruct
    states = (plan.depth - 1, plan.span, plan.channels)
    return pl.pallas_call(
        functools.partial(forward_kernel, plan=plan),
        out_shape=(shape(states, BF16), *[shape((plan.share, plan.channels), BF16)] * plan.depth),
        in_specs=[IN_SMEM] + [ANYWHERE] * (len(stacks) + 1) + [IN_VMEM] * 4,
        out_specs=(ANYWHERE,) * (plan.depth + 1),
        scratch_shapes=[
            pltpu.VMEM((2, plan.channels, plan.channels), BF16),
            pltpu.VMEM((plan.span, plan.channels), BF16),
            pltpu.VMEM(states, BF16),
            pltpu.VMEM((plan.depth, plan.share, plan.channels), BF16),
            pltpu.VMEM((plan.span, plan.channels), BF16),
            pltpu.VMEM((plan.held, 4, plan.tok, plan.head), F32),
            pltpu.SemaphoreType.DMA((2, plan.ways)),
            pltpu.SemaphoreType.DMA((1,)),
            pltpu.SemaphoreType.DMA((plan.depth - 1,)),
            pltpu.SemaphoreType.DMA((plan.depth,)),
        ],
        name="forward",
        **params(2 * plan.depth * plan.span * plan.channels * plan.channels, 2 * plan.depth * plan.channels**2),
    )(scalars, *stacks, rows, cos, sin, gains, swap)


def back_kernel(scalars, *refs, plan, phases):
    stacks, refs = refs[: plan.pieces], refs[plan.pieces :]
    states, grad_any, cos_ref, sin_ref, gains, swap_ref = refs[:6]
    top, count = phases[0], len(phases)
    grad_out, gain_out, sent_out, refs = refs[6], refs[7], refs[8 : 8 + count], refs[8 + count :]
    buffer, hidden, sent, grad_mixed, tables, sums, sems, state_sems, row_sem, sent_sems = refs
    base = scalars[plan.base_at]
    counts = [scalars[plan.counts_at + t].astype(F32) for t in range(plan.held)]
    source = grad_any.at[own_rows(plan, scalars)] if top == plan.depth - 1 else grad_any
    load = pltpu.make_async_copy(source, grad_out, row_sem.at[0])
    load.start()

    def fetch(phase):
        slot = phase % 2
        waits = load_weight(plan, scalars, stacks, phase, buffer.at[slot], sems.at[slot])
        waits.append(pltpu.make_async_copy(states.at[phase - 1], hidden.at[slot], state_sems.at[slot]))
        waits[-1].start()
        return waits

    coming = {phase: fetch(phase) for phase in phases[:2]}
    load.wait()
    going = []
    for i, phase in enumerate(phases):
        slot = phase % 2
        fill_tables(tables, cos_ref, sin_ref, gains.at[scalars[plan.place_at] ^ phase], swap_ref, base)
        wait_all(coming[phase])
        pull_mixed(grad_out, buffer.at[slot], grad_mixed, plan.width)
        gain_out[i] = pull_rows(
            hidden.at[slot], grad_out, grad_mixed, tables, cos_ref, sin_ref, base, gains.at[scalars[plan.place_at] ^ phase], swap_ref, counts,
            sums, grad_out, plan.tok, plan.head, plan.heads,
        )
        sent[i] = grad_out[window_of(plan, scalars), :]
        going.append(pltpu.make_async_copy(sent.at[i], sent_out[i], sent_sems.at[i]))
        going[-1].start()
        if phase - 2 in phases:
            coming[phase - 2] = fetch(phase - 2)
    wait_all(going)


def back(plan, phases, scalars, stacks, states, grad, cos, sin, gains, swap):
    shape = jax.ShapeDtypeStruct
    count = len(phases)
    return pl.pallas_call(
        functools.partial(back_kernel, plan=plan, phases=phases),
        out_shape=(
            shape((plan.span, plan.channels), BF16),
            shape((count, GAIN_ROWS, plan.head), F32),
            *[shape((plan.share, plan.channels), BF16)] * count,
        ),
        in_specs=[IN_SMEM] + [ANYWHERE] * (len(stacks) + 2) + [IN_VMEM] * 4,
        out_specs=(IN_VMEM, IN_VMEM, *[ANYWHERE] * count),
        scratch_shapes=[
            pltpu.VMEM((2, plan.channels, plan.channels), BF16),
            pltpu.VMEM((2, plan.span, plan.channels), BF16),
            pltpu.VMEM((count, plan.share, plan.channels), BF16),
            pltpu.VMEM((plan.span, plan.channels), BF16),
            pltpu.VMEM((plan.held, 8, plan.tok, plan.head), F32),
            pltpu.VMEM((plan.held, 2, plan.tok, plan.head), F32),
            pltpu.SemaphoreType.DMA((2, plan.ways)),
            pltpu.SemaphoreType.DMA((2,)),
            pltpu.SemaphoreType.DMA((1,)),
            pltpu.SemaphoreType.DMA((count,)),
        ],
        name="back",
        **params(6 * count * plan.span * plan.channels * plan.channels, 3 * count * plan.channels**2),
    )(scalars, *stacks, states, grad, cos, sin, gains, swap)


def first_back_kernel(scalars, *refs, plan):
    stacks, refs = refs[: plan.pieces], refs[plan.pieces :]
    rows, grad_any, cos_ref, sin_ref, gains, swap_ref, gain_out = refs[:7]
    buffer, hidden, grad_in, grad_mixed, tables, sums, sems, row_sems = refs[7:]
    base = scalars[plan.base_at]
    counts = [scalars[plan.counts_at + t].astype(F32) for t in range(plan.held)]
    copies = [
        pltpu.make_async_copy(grad_any, grad_in, row_sems.at[0]),
        pltpu.make_async_copy(rows.at[own_rows(plan, scalars)], hidden, row_sems.at[1]),
    ]
    start_all(copies)
    copies += load_weight(plan, scalars, stacks, 0, buffer, sems)
    fill_tables(tables, cos_ref, sin_ref, gains.at[scalars[plan.place_at]], swap_ref, base)
    wait_all(copies)
    pull_mixed(grad_in, buffer, grad_mixed, plan.width)
    gain_out[...] = pull_rows(
        hidden, grad_in, grad_mixed, tables, cos_ref, sin_ref, base, gains.at[scalars[plan.place_at]], swap_ref, counts, sums, None,
        plan.tok, plan.head, plan.heads,
    )


def first_back(plan, scalars, stacks, rows, grad_in, cos, sin, gains, swap):
    held = pltpu.VMEM((plan.span, plan.channels), BF16)
    return pl.pallas_call(
        functools.partial(first_back_kernel, plan=plan),
        out_shape=jax.ShapeDtypeStruct((GAIN_ROWS, plan.head), F32),
        in_specs=[IN_SMEM] + [ANYWHERE] * (len(stacks) + 2) + [IN_VMEM] * 4,
        out_specs=IN_VMEM,
        scratch_shapes=[
            pltpu.VMEM((plan.channels, plan.channels), BF16),
            held,
            held,
            held,
            pltpu.VMEM((plan.held, 8, plan.tok, plan.head), F32),
            pltpu.VMEM((plan.held, 2, plan.tok, plan.head), F32),
            pltpu.SemaphoreType.DMA((plan.ways,)),
            pltpu.SemaphoreType.DMA((2,)),
        ],
        name="first_back",
        **params(6 * plan.span * plan.channels * plan.channels, 3 * plan.channels**2),
    )(scalars, *stacks, rows, grad_in, cos, sin, gains, swap)


def turn_kernel(place, *refs, plan):
    count = 2 * plan.depth - 1
    sets = [refs[:count], refs[count : 2 * count]]
    out, gathered, turned, sems = refs[2 * count :]
    copies = []
    for half, (own, received) in enumerate((x[: plan.depth], x[plan.depth :]) for x in sets):
        for k in range(plan.depth):
            at = half * plan.depth + k
            rows = gathered.at[pl.ds(at * plan.share, plan.share)]
            if k:
                copies.append(pltpu.make_async_copy(received[k - 1], rows, sems.at[at]))
                copies[-1].start()
            else:
                for phase in range(plan.depth):
                    copy = pltpu.make_async_copy(own[phase], rows, sems.at[at])
                    pl.when(place[0] == phase)(copy.start)
                copies.append(copy)
    wait_all(copies)

    def part(i, carry):
        cols = pl.ds(pl.multiple_of(i * plan.width, plan.width), plan.width)
        turned[cols, :] = gathered[:, cols].T
        return carry

    lax.fori_loop(0, plan.channels // plan.width, part, 0)
    for k in range(plan.chips):
        start = ((place[2] ^ k) * CORES + place[1]) * plan.rows
        out[k] = turned[pl.ds(pl.multiple_of(start, math.gcd(plan.rows, 16)), plan.rows), :]


def turn(plan, place, own, received, own_other, received_other):
    total = 2 * plan.depth * plan.share
    return pl.pallas_call(
        functools.partial(turn_kernel, plan=plan),
        out_shape=jax.ShapeDtypeStruct((plan.chips, plan.rows, total), BF16),
        in_specs=[IN_SMEM] + [ANYWHERE] * (4 * plan.depth - 2),
        out_specs=IN_VMEM,
        scratch_shapes=[
            pltpu.VMEM((total, plan.channels), BF16),
            pltpu.VMEM((plan.channels, total), BF16),
            pltpu.SemaphoreType.DMA((2 * plan.depth,)),
        ],
        name="turn",
        **params(0, 4 * total * plan.channels),
    )(place, *own, *received, *own_other, *received_other)


def term_kernel(place, gain_ref, turned_any, cot, cot_other, *refs, plan, half):
    count = 2 * plan.depth - 2
    sets, refs = [refs[:count], refs[count : 2 * count]], refs[2 * count :]
    outs, (turned, grads, terms, extra, sems, turned_sem, out_sems, extra_sems) = refs[: plan.chips], refs[plan.chips :]
    total = 2 * plan.depth
    width = plan.channels // 4
    chunks = [pl.ds((2 * half + i) * width, width) for i in range(2)]
    load = pltpu.make_async_copy(turned_any, turned, turned_sem.at[0])
    load.start()

    def gather(phase):
        for i, cols in enumerate(chunks):
            for at in range(total):
                side, k = divmod(at, plan.depth)
                if phase == plan.depth - 1:
                    source = (cot, cot_other)[side].at[pl.ds((phase ^ k) * plan.share, plan.share), cols]
                else:
                    source = (sets[side][plan.depth - 2 + k] if k else sets[side][phase]).at[:, cols]
                target = grads.at[i, pl.ds(at * plan.share, plan.share)]
                pltpu.make_async_copy(source, target, sems.at[i, at]).start()

    for phase in range(plan.depth):
        pl.when(place[0] == phase)(functools.partial(gather, phase))
    going = []
    if half:
        extra[...] = jnp.zeros(extra.shape, BF16)
        left = gain_ref[...]
        for i in range(GAIN_PARTS):
            part = left.astype(BF16)
            extra[0:GAIN_ROWS, i * plan.head : (i + 1) * plan.head] = part
            left = left - part.astype(F32)
        for k in range(plan.chips):
            target = outs[k].at[pl.ds(plan.rows, EXTRA_ROWS)]
            going.append(pltpu.make_async_copy(extra, target, extra_sems.at[k]))
            going[-1].start()
    load.wait()
    for i, cols in enumerate(chunks):
        for at in range(total):
            rows = grads.at[i, pl.ds(at * plan.share, plan.share)]
            pltpu.make_async_copy(rows, rows, sems.at[i, at]).wait()
        for k in range(plan.chips):
            terms[i, k] = jnp.dot(turned[k], grads[i], preferred_element_type=F32).astype(BF16)
            target = outs[k].at[pl.ds(0, plan.rows), pl.ds(i * width, width)]
            going.append(pltpu.make_async_copy(terms.at[i, k], target, out_sems.at[i, k]))
            going[-1].start()
    wait_all(going)


def term(plan, half, place, gain, turned, cot, cot_other, windows, received, windows_other, received_other):
    total = 2 * plan.depth * plan.share
    width = plan.channels // 4
    given = [*windows, *received, *windows_other, *received_other]
    return pl.pallas_call(
        functools.partial(term_kernel, plan=plan, half=half),
        out_shape=[jax.ShapeDtypeStruct((plan.rows + (EXTRA_ROWS if half else 0), 2 * width), BF16)] * plan.chips,
        in_specs=[IN_SMEM, IN_VMEM] + [ANYWHERE] * (3 + len(given)),
        out_specs=[ANYWHERE] * plan.chips,
        scratch_shapes=[
            pltpu.VMEM((plan.chips, plan.rows, total), BF16),
            pltpu.VMEM((2, total, width), BF16),
            pltpu.VMEM((2, plan.chips, plan.rows, width), BF16),
            pltpu.VMEM((EXTRA_ROWS, 2 * width), BF16),
            pltpu.SemaphoreType.DMA((2, 2 * plan.depth)),
            pltpu.SemaphoreType.DMA((1,)),
            pltpu.SemaphoreType.DMA((2, plan.chips)),
            pltpu.SemaphoreType.DMA((plan.chips,)),
        ],
        name="term",
        **params(total * plan.channels**2, 4 * plan.channels**2),
    )(place, gain, turned, cot, cot_other, *given)


def along_pipe(x, k):
    return lax.ppermute(x, "pipe", [(i, i ^ k) for i in range(lax.axis_size("pipe"))])


def along_chips(x, k):
    return lax.ppermute(x, "dp", [(i, i ^ (CORES * k)) for i in range(lax.axis_size("dp"))])


def other_core(x):
    return lax.ppermute(x, "dp", [(i, i ^ 1) for i in range(lax.axis_size("dp"))])


def spread_near(block, depth):
    return {1 << bit: along_pipe(block, 1 << bit) for bit in range(depth.bit_length() - 1)}


def spread_far(near, depth):
    bits = depth.bit_length() - 1
    part = near[1].shape[0] // bits
    got = {k: [x[i * part : (i + 1) * part] for i in range(bits)] for k, x in near.items()}
    for k in sorted(range(1, depth), key=lambda k: k.bit_count()):
        if k not in got:
            got[k] = []
            for i in range(bits):
                order = [(i + b) % bits for b in range(bits)]
                bit = 1 << [b for b in order if k >> b & 1][-1]
                got[k].append(along_pipe(got[k ^ bit][i], bit))
    return {k: parts for k, parts in got.items() if k not in near}


def gather_weights(plan, own, gain, chip, beside):
    chips, depth = plan.chips, plan.depth
    order = [sorted((b for b in range(chips) if b != c), key=lambda b: (abs(b - c), b ^ c)) for c in range(chips)]
    up = down = block = own
    arrived = {}
    ours, nears, theirs, gains, extra = [], [], [], (), ()

    def swapped(i, keys):
        return {k: [other_core(x) for x in ours[i][k]] for k in keys}

    near_keys = [k for k in range(depth) if k.bit_count() < 2]
    far_keys = [k for k in range(depth) if k.bit_count() > 1]

    for step in range(1, chips + 1):
        near = spread_near(block, depth)
        if step == 1:
            gains = [along_pipe(gain, k) for k in range(1, depth)]
        if step == 2:
            extra = beside(jnp.asarray([[c, *order[c]] for c in range(chips)], jnp.int32)[chip])
        far = spread_far(nears[-1], depth) if step > 1 else {}
        swaps = []
        if step > 2:
            swaps = [swapped(step - 3, range(depth))]
        if step < chips:
            up = lax.ppermute(up, "dp", [(i, i + CORES) for i in range(plan.ways - CORES)])
            down = lax.ppermute(down, "dp", [(i + CORES, i) for i in range(plan.ways - CORES)])
        up, down, near, gains, extra, swaps = lax.optimization_barrier(
            (up, down, near, gains, extra, swaps)
        )
        theirs += swaps
        if step > 1:
            ours[-1].update(far)
        nears.append(near)
        ours.append({0: [block], **{k: [x] for k, x in near.items()}})
        arrived[step, -1], arrived[step, 1] = up, down
        if step < chips:
            places = {}
            for c in range(chips):
                b = order[c][step - 1]
                places.setdefault((abs(b - c), 1 if b > c else -1), []).append(c)
            (first, _), *rest = places.items()
            block = arrived[first]
            for key, members in rest:
                here = functools.reduce(jnp.logical_or, [chip == c for c in members])
                block = jnp.where(here, arrived[key], block)
    far = spread_far(nears[-1], depth)
    left = [swapped(i, range(depth)) for i in range(len(theirs), chips - 1)] + [swapped(chips - 1, near_keys)]
    ours[-1].update(far)
    theirs += left
    theirs[-1].update(swapped(chips - 1, far_keys))
    pieces = [x for block in ours + theirs for k in range(depth) for x in block[k]]
    return pieces, jnp.stack([gain, *gains]).astype(F32), extra


def shards(clips, positions, out_proj, qk_gains, cotangent):
    plan = Plan(clips, out_proj, qk_gains)
    depth, last = plan.depth, plan.depth - 1
    place = lax.axis_index("pipe")
    member = lax.axis_index("dp")
    chip, core = member // CORES, member % CORES
    rows = clips.reshape(plan.tiles * plan.tok, plan.channels)
    last_grad = cotangent.reshape(plan.tiles * plan.tok, plan.channels)
    coord, freq, sign, partner = lane_tables(plan.head)
    own_gain = jnp.pad(qk_gains[0], ((0, GAIN_ROWS - 2), (0, 0)))
    first_row = place * plan.share
    base = jnp.minimum(first_row // plan.tok, plan.tiles - plan.held)
    tile_starts = (base + jnp.arange(plan.held)) * plan.tok
    counts = ((tile_starts >= first_row) & (tile_starts < first_row + plan.share)).astype(jnp.int32)

    def settings(whose):
        spots = positions.reshape(3, plan.tiles, plan.tok, 1).astype(F32)
        angle = jnp.where(coord == 0, spots[0], jnp.where(coord == 1, spots[1], spots[2])) * freq
        swap = jnp.asarray(np.eye(plan.head)[partner], BF16)
        starts = [(whose * CORES + core) * plan.rows, (whose * CORES + 1 - core) * plan.rows]
        more = jnp.stack([base, first_row - base * plan.tok, place])
        scalars = jnp.concatenate([*starts, more, counts]).astype(jnp.int32)
        return scalars, jnp.cos(angle), jnp.sin(angle) * sign, swap

    blocks, gains, (scalars, cos, sin, swap) = gather_weights(plan, out_proj[0], own_gain, chip, settings)
    setting = (cos, sin, gains, swap)

    def to_owners(windows):
        got = []
        for k in range(1, depth):
            chosen = windows[0]
            for phase in range(1, len(windows)):
                chosen = jnp.where(place ^ k == phase, windows[phase], chosen)
            got.append(lax.ppermute(chosen, "pipe", [(i, i ^ k) for i in range(depth) if i ^ k < len(windows)]))
        return got

    states, *mixed = forward(plan, scalars, blocks, rows, *setting)
    received = to_owners(mixed)
    near = [k - 1 for k in range(1, depth) if k.bit_count() == 1]
    far = [k - 1 for k in range(1, depth) if k.bit_count() > 1]
    grad, terms, windows = last_grad, [], []
    upper = range(last, 1, -1)
    if upper:
        grad, gain, *windows = back(plan, upper, scalars, blocks, states, grad, *setting)
        terms.append(gain)
    mixed_other, cot_other = [other_core(x) for x in mixed], other_core(last_grad)
    grad, arrived, mixed_other, cot_other = lax.optimization_barrier(
        (grad, [received[i] for i in near], mixed_other, cot_other)
    )
    for i, x in zip(near, arrived):
        received[i] = x
    received_other = {i: other_core(received[i]) for i in near}
    windows_other = [other_core(x) for x in windows]
    grad, gain, window = back(plan, range(1, 0, -1), scalars, blocks, states, grad, *setting)
    grad, window, arrived, received_other, windows_other = lax.optimization_barrier(
        (grad, window, [received[i] for i in far], received_other, windows_other)
    )
    for i, x in zip(far, arrived):
        received[i] = x
    windows = [window, *reversed(windows)]
    terms = jnp.concatenate([*terms, gain], axis=0)[::-1]
    grads = to_owners(windows)
    first_term = first_back(plan, scalars, blocks, rows, grad, *setting)
    where = jnp.stack([place, core, chip]).astype(jnp.int32)
    received_other.update({i: other_core(received[i]) for i in far})
    windows_other = [other_core(window), *reversed(windows_other)]
    turned = turn(plan, where, mixed, received, mixed_other, [received_other[i] for i in range(last)])
    turned, windows_other, first_term, arrived = lax.optimization_barrier(
        (turned, windows_other, first_term, [grads[i] for i in far])
    )
    for i, x in zip(far, arrived):
        grads[i] = x

    grads_other = [other_core(x) for x in grads]
    given = (turned, last_grad, cot_other, windows, grads, windows_other, grads_other)
    terms = jnp.concatenate([first_term[None], terms], axis=0)
    totals, gain_sum = [], first_term
    for half in range(2):
        if half:
            pieces[0], terms = lax.optimization_barrier((pieces[0], terms))
            gain_sum = lax.dynamic_index_in_dim(terms, place, 0, keepdims=False)
            for k in range(1, depth):
                sent = lax.dynamic_index_in_dim(terms, place ^ k, 0, keepdims=False)
                gain_sum = gain_sum + along_pipe(sent, k)
            gain_sum = gain_sum + other_core(gain_sum)
        pieces = list(term(plan, half, where, gain_sum, *given))
        parts = [pieces[0], *[along_chips(pieces[k], k) for k in range(1, plan.chips)]]
        totals.append(sum(part[: plan.rows].astype(F32) for part in parts))
    by_chip = jnp.stack([part[plan.rows : plan.rows + 2] for part in parts])[chip ^ jnp.arange(plan.chips)]
    gain_parts = jnp.sum(by_chip.astype(F32), axis=0)
    own_gains = sum(gain_parts[:, i * plan.head : (i + 1) * plan.head] for i in range(GAIN_PARTS))
    return (jnp.concatenate(totals, axis=1)[None], own_gains[None])


def solution(mesh):
    placed = (
        P(None, None, "dp", None),
        P(None, None, None, "dp"),
        P("pipe", "dp", None),
        P("pipe", None, None),
        P(None, None, "dp", None),
    )
    return jax.shard_map(
        shards,
        mesh=mesh,
        in_specs=placed,
        out_specs=(P("pipe", "dp", None), P("pipe", None, None)),
        check_vma=False,
    )
```

```python
import functools
import math

import jax
import jax.numpy as jnp
import numpy as np
from jax import lax
from jax.experimental import pallas as pl
from jax.experimental.pallas import tpu as pltpu
from jax.sharding import PartitionSpec as P

F32 = jnp.float32
BF16 = jnp.bfloat16
VMEM_BYTES = 56 * 1024 * 1024
CORES = 2
GAIN_ROWS = 8
GAIN_PARTS = 3
EXTRA_ROWS = 16


def lane_tables(head):
    first = head // 8
    rest = (head - first) // 2
    coord = np.zeros(head, np.int32)
    freq = np.zeros(head, np.float32)
    sign = np.zeros(head, np.float32)
    partner = np.zeros(head, np.int32)
    offset = 0
    for axis, width in enumerate((first, rest, rest)):
        half = width // 2
        for j in range(half):
            low, high = offset + j, offset + j + half
            coord[low] = coord[high] = axis
            freq[low] = freq[high] = 256.0 ** (-2.0 * j / width)
            sign[low], sign[high] = -1.0, 1.0
            partner[low], partner[high] = high, low
        offset += width
    return coord, freq, sign, partner


def nt(a, b):
    return lax.dot_general(a, b, (((1,), (1,)), ((), ())), preferred_element_type=F32)


def tn(a, b):
    return lax.dot_general(a, b, (((0,), (0,)), ((), ())), preferred_element_type=F32)


def split(x):
    high = x.astype(BF16)
    return high, (x - high.astype(F32)).astype(BF16)


def fill_tables(tables, cos_ref, sin_ref, gain_ref, swap_ref, first=0):
    gain = gain_ref[...]
    turned = jnp.dot(gain.astype(BF16), swap_ref[...], preferred_element_type=F32)
    factor = 1.0 / math.sqrt(gain.shape[-1])
    query, query_turned, key, key_turned = gain[0:1] * factor, turned[0:1] * factor, gain[1:2], turned[1:2]
    for t in range(tables.shape[0]):
        cosine, sine = cos_ref[first + t], sin_ref[first + t]
        tables[t, 0] = cosine * query
        tables[t, 1] = sine * query_turned
        tables[t, 2] = cosine * key
        tables[t, 3] = sine * key_turned
        if tables.shape[1] > 4:
            tables[t, 4] = cosine * query_turned
            tables[t, 5] = -sine * query
            tables[t, 6] = cosine * key_turned
            tables[t, 7] = -sine * key


def project(hidden, mixed, weight, out, width):
    def part(i, carry):
        cols = pl.ds(pl.multiple_of(i * width, width), width)
        update = jnp.dot(mixed[...], weight[:, cols], preferred_element_type=F32)
        out[:, cols] = (hidden[:, cols].astype(F32) + update).astype(BF16)
        return carry

    lax.fori_loop(0, out.shape[1] // width, part, 0)


def pull_mixed(grad, weight, grad_mixed, width):
    def part(i, carry):
        cols = pl.ds(pl.multiple_of(i * width, width), width)
        grad_mixed[:, cols] = nt(grad[...], weight[cols, :]).astype(BF16)
        return carry

    lax.fori_loop(0, grad_mixed.shape[1] // width, part, 0)


def head_stage(pairs, hidden, tables, swap):
    values = [hidden[r, c] for _, r, c in pairs]
    wide = [v.astype(F32) for v in values]
    scale = [lax.rsqrt(jnp.mean(x * x, axis=-1, keepdims=True) + 1e-06) for x in wide]
    turned = [jnp.dot(v, swap, preferred_element_type=F32) * s for v, s in zip(values, scale)]
    normed = [x * s for x, s in zip(wide, scale)]
    queries = [split(n * tables[t, 0] + w * tables[t, 1]) for (t, _, _), n, w in zip(pairs, normed, turned)]
    keys = [split(n * tables[t, 2] + w * tables[t, 3]) for (t, _, _), n, w in zip(pairs, normed, turned)]
    scores = [
        nt(jnp.concatenate([qh, ql, qh], axis=1), jnp.concatenate([kh, kh, kl], axis=1))
        for (qh, ql), (kh, kl) in zip(queries, keys)
    ]
    raised = [jnp.exp(s) for s in scores]
    weights = [e * (1.0 / jnp.sum(e, axis=-1, keepdims=True)) for e in raised]
    return values, normed, turned, scale, [q[0] for q in queries], [k[0] for k in keys], weights


def head_pairs(step, groups, tok, head, together):
    cols = [pl.ds(pl.multiple_of((step * together + u) * head, head), head) for u in range(together)]
    return [(t, slice(t * tok, (t + 1) * tok), c) for c in cols for t in range(groups)]


def mix_rows(hidden, tables, swap_ref, mixed, tok, head, together):
    groups = hidden.shape[0] // tok
    swap = swap_ref[...]

    def some(i, carry):
        pairs = head_pairs(i, groups, tok, head, together)
        values, _, _, _, _, _, weights = head_stage(pairs, hidden, tables, swap)
        rounded = [w.astype(BF16) for w in weights]
        results = [jnp.dot(w, v, preferred_element_type=F32).astype(BF16) for w, v in zip(rounded, values)]
        for (_, r, c), m in zip(pairs, results):
            mixed[r, c] = m
        return carry

    lax.fori_loop(0, hidden.shape[1] // head // together, some, 0)


def pull_rows(
    hidden, grad, grad_mixed, tables, cos_ref, sin_ref, first, gain_ref, swap_ref, counts, sums, out, tok, head, together
):
    groups = hidden.shape[0] // tok
    swap = swap_ref[...]
    factor = 1.0 / math.sqrt(head)
    gain_q, gain_k = gain_ref[0:1, :] * factor, gain_ref[1:2, :]
    sums[...] = jnp.zeros(sums.shape, F32)

    def some(i, carry):
        pairs = head_pairs(i, groups, tok, head, together)
        values, normed, turned, scale, queries, keys, weights = head_stage(pairs, hidden, tables, swap)
        queries = [
            jnp.concatenate([q, (w * tables[t, 4] + n * tables[t, 5]).astype(BF16)], axis=1)
            for (t, _, _), q, n, w in zip(pairs, queries, normed, turned)
        ]
        keys = [
            jnp.concatenate([k, (w * tables[t, 6] + n * tables[t, 7]).astype(BF16)], axis=1)
            for (t, _, _), k, n, w in zip(pairs, keys, normed, turned)
        ]
        above = [grad_mixed[r, c] for _, r, c in pairs]
        grad_weights = [nt(a, v).astype(BF16).astype(F32) for a, v in zip(above, values)]
        if out is not None:
            grad_values = [tn(w.astype(BF16), a) for w, a in zip(weights, above)]
        means = [jnp.sum(g * w, axis=-1, keepdims=True) for g, w in zip(grad_weights, weights)]
        grad_scores = [(w * (g - m)).astype(BF16) for w, g, m in zip(weights, grad_weights, means)]
        grad_q = [jnp.dot(s, k, preferred_element_type=F32) for s, k in zip(grad_scores, keys)]
        grad_k = [tn(s, q) for s, q in zip(grad_scores, queries)]
        back_q = [g[:, :head] * cos_ref[first + p[0]] - g[:, head:] * sin_ref[first + p[0]] for p, g in zip(pairs, grad_q)]
        back_k = [g[:, :head] * cos_ref[first + p[0]] - g[:, head:] * sin_ref[first + p[0]] for p, g in zip(pairs, grad_k)]
        for t in range(groups):
            mine = [j for j, p in enumerate(pairs) if p[0] == t]
            sums[t, 0] += sum(normed[j] * back_q[j] for j in mine)
            sums[t, 1] += sum(normed[j] * back_k[j] for j in mine)
        if out is not None:
            grad_normed = [q * gain_q + k * gain_k for q, k in zip(back_q, back_k)]
            along = [jnp.mean(n * g, axis=-1, keepdims=True) for n, g in zip(normed, grad_normed)]
            grad_hidden = [
                (v + s * (g - n * a)).astype(BF16).astype(F32)
                for v, s, g, n, a in zip(grad_values, scale, grad_normed, normed, along)
            ]
            for (_, r, c), g in zip(pairs, grad_hidden):
                out[r, c] = (grad[r, c].astype(F32) + g).astype(BF16)
        return carry

    lax.fori_loop(0, hidden.shape[1] // head // together, some, 0)
    total = [
        sum(counts[t] * jnp.sum(sums[t, i], axis=0, keepdims=True) for t in range(groups)) for i in range(2)
    ]
    return jnp.concatenate([total[0] * factor, total[1], jnp.zeros((GAIN_ROWS - 2, head), F32)], axis=0)


def params(flops, size):
    return dict(
        compiler_params=pltpu.CompilerParams(vmem_limit_bytes=VMEM_BYTES),
        cost_estimate=pl.CostEstimate(flops=flops, bytes_accessed=size, transcendentals=0),
    )


IN_VMEM = pl.BlockSpec(memory_space=pltpu.VMEM)
IN_SMEM = pl.BlockSpec(memory_space=pltpu.SMEM)
ANYWHERE = pl.BlockSpec(memory_space=pl.ANY)


class Plan:
    def parts_of(self, k):
        return 1 if k.bit_count() < 2 else self.depth.bit_length() - 1

    def __init__(self, clips, out_proj, qk_gains):
        self.depth = lax.axis_size("pipe")
        self.ways = lax.axis_size("dp")
        self.tok = clips.shape[2]
        self.channels = clips.shape[3]
        self.head = qk_gains.shape[-1]
        self.heads = self.channels // self.head
        self.tiles = clips.shape[0] * clips.shape[1]
        self.rows = out_proj.shape[1]
        self.share = self.tiles * self.tok // self.depth
        self.held = max(-(-(p * self.share % self.tok + self.share) // self.tok) for p in range(self.depth))
        self.span = self.held * self.tok
        self.width = math.gcd(self.channels, 512)
        self.chips = self.ways // CORES
        self.base_at = self.ways
        self.pieces = self.ways * sum(self.parts_of(k) for k in range(self.depth))
        self.window_at = self.base_at + 1
        self.place_at = self.base_at + 2
        self.counts_at = self.base_at + 3


def load_weight(plan, scalars, pieces, phase, buffer, sems):
    waits = []
    refs = iter(pieces)
    for i in range(plan.ways):
        first = scalars[i]
        for k in range(plan.depth):
            parts = plan.parts_of(k)
            size = plan.rows // parts
            copies = []
            for j in range(parts):
                rows = pl.ds(pl.multiple_of(first + j * size, math.gcd(size, 16)), size)
                copies.append(pltpu.make_async_copy(next(refs), buffer.at[rows], sems.at[i]))
            pl.when(scalars[plan.place_at] == phase ^ k)(functools.partial(start_all, copies))
        rows = buffer.at[pl.ds(pl.multiple_of(first, math.gcd(plan.rows, 16)), plan.rows)]
        waits.append(pltpu.make_async_copy(rows, rows, sems.at[i]))
    return waits


def start_all(copies):
    for copy in copies:
        copy.start()


def wait_all(copies):
    for copy in copies:
        copy.wait()


def window_of(plan, scalars):
    return pl.ds(pl.multiple_of(scalars[plan.window_at], math.gcd(plan.share, plan.tok)), plan.share)


def own_rows(plan, scalars):
    return pl.ds(pl.multiple_of(scalars[plan.base_at] * plan.tok, plan.tok), plan.span)


def to_owner(plan, scalars, phase, rows, outs, sem):
    for k, out in enumerate(outs):
        copy = pltpu.make_async_copy(rows, out, sem)
        pl.when(scalars[plan.place_at] == phase ^ k)(copy.start)
    return copy


def forward_kernel(scalars, *refs, plan):
    stacks, refs = refs[: plan.pieces], refs[plan.pieces :]
    rows, cos_ref, sin_ref, gains, swap_ref = refs[:5]
    states_out, sent_out, refs = refs[5], refs[6 : 6 + plan.depth], refs[6 + plan.depth :]
    buffer, start, states, sent, mixed, tables, sems, row_sem, state_sems, sent_sems = refs
    last = plan.depth - 1
    base = scalars[plan.base_at]
    load = pltpu.make_async_copy(rows.at[own_rows(plan, scalars)], start, row_sem.at[0])
    load.start()

    def fetch(phase):
        return load_weight(plan, scalars, stacks, phase, buffer.at[phase % 2], sems.at[phase % 2])

    coming = {phase: fetch(phase) for phase in range(min(2, last))}
    going = []
    for phase in range(plan.depth):
        hidden = states.at[phase - 1] if phase else start
        fill_tables(tables, cos_ref, sin_ref, gains.at[scalars[plan.place_at] ^ phase], swap_ref, base)
        if phase == 0:
            load.wait()
        mix_rows(hidden, tables, swap_ref, mixed, plan.tok, plan.head, plan.heads)
        sent[phase] = mixed[window_of(plan, scalars), :]
        going.append(to_owner(plan, scalars, phase, sent.at[phase], sent_out, sent_sems.at[phase]))
        if phase < last:
            wait_all(coming[phase])
            project(hidden, mixed, buffer.at[phase % 2], states.at[phase], plan.width)
            going.append(pltpu.make_async_copy(states.at[phase], states_out.at[phase], state_sems.at[phase]))
            going[-1].start()
            if phase + 2 < last:
                coming[phase + 2] = fetch(phase + 2)
    wait_all(going)


def forward(plan, scalars, stacks, rows, cos, sin, gains, swap):
    shape = jax.ShapeDtypeStruct
    states = (plan.depth - 1, plan.span, plan.channels)
    return pl.pallas_call(
        functools.partial(forward_kernel, plan=plan),
        out_shape=(shape(states, BF16), *[shape((plan.share, plan.channels), BF16)] * plan.depth),
        in_specs=[IN_SMEM] + [ANYWHERE] * (len(stacks) + 1) + [IN_VMEM] * 4,
        out_specs=(ANYWHERE,) * (plan.depth + 1),
        scratch_shapes=[
            pltpu.VMEM((2, plan.channels, plan.channels), BF16),
            pltpu.VMEM((plan.span, plan.channels), BF16),
            pltpu.VMEM(states, BF16),
            pltpu.VMEM((plan.depth, plan.share, plan.channels), BF16),
            pltpu.VMEM((plan.span, plan.channels), BF16),
            pltpu.VMEM((plan.held, 4, plan.tok, plan.head), F32),
            pltpu.SemaphoreType.DMA((2, plan.ways)),
            pltpu.SemaphoreType.DMA((1,)),
            pltpu.SemaphoreType.DMA((plan.depth - 1,)),
            pltpu.SemaphoreType.DMA((plan.depth,)),
        ],
        name="forward",
        **params(2 * plan.depth * plan.span * plan.channels * plan.channels, 2 * plan.depth * plan.channels**2),
    )(scalars, *stacks, rows, cos, sin, gains, swap)


def back_kernel(scalars, *refs, plan, phases):
    stacks, refs = refs[: plan.pieces], refs[plan.pieces :]
    states, grad_any, cos_ref, sin_ref, gains, swap_ref = refs[:6]
    top, count = phases[0], len(phases)
    outs = plan.depth
    grad_out, gain_out, sent_out, refs = refs[6], refs[7], refs[8 : 8 + outs], refs[8 + outs :]
    buffer, hidden, sent, grad_mixed, tables, sums, sems, state_sems, row_sem, sent_sems = refs
    base = scalars[plan.base_at]
    counts = [scalars[plan.counts_at + t].astype(F32) for t in range(plan.held)]
    source = grad_any.at[own_rows(plan, scalars)] if top == plan.depth - 1 else grad_any
    load = pltpu.make_async_copy(source, grad_out, row_sem.at[0])
    load.start()

    def fetch(phase):
        slot = phase % 2
        waits = load_weight(plan, scalars, stacks, phase, buffer.at[slot], sems.at[slot])
        waits.append(pltpu.make_async_copy(states.at[phase - 1], hidden.at[slot], state_sems.at[slot]))
        waits[-1].start()
        return waits

    coming = {phase: fetch(phase) for phase in phases[:2]}
    load.wait()
    going = []
    for i, phase in enumerate(phases):
        slot = phase % 2
        fill_tables(tables, cos_ref, sin_ref, gains.at[scalars[plan.place_at] ^ phase], swap_ref, base)
        wait_all(coming[phase])
        pull_mixed(grad_out, buffer.at[slot], grad_mixed, plan.width)
        gain_out[i] = pull_rows(
            hidden.at[slot], grad_out, grad_mixed, tables, cos_ref, sin_ref, base, gains.at[scalars[plan.place_at] ^ phase], swap_ref, counts,
            sums, grad_out, plan.tok, plan.head, plan.heads,
        )
        sent[i] = grad_out[window_of(plan, scalars), :]
        going.append(to_owner(plan, scalars, phase - 1, sent.at[i], sent_out, sent_sems.at[i]))
        if phase - 2 in phases:
            coming[phase - 2] = fetch(phase - 2)
    wait_all(going)


def back(plan, phases, scalars, stacks, states, grad, cos, sin, gains, swap):
    shape = jax.ShapeDtypeStruct
    count = len(phases)
    outs = plan.depth
    return pl.pallas_call(
        functools.partial(back_kernel, plan=plan, phases=phases),
        out_shape=(
            shape((plan.span, plan.channels), BF16),
            shape((count, GAIN_ROWS, plan.head), F32),
            *[shape((plan.share, plan.channels), BF16)] * outs,
        ),
        in_specs=[IN_SMEM] + [ANYWHERE] * (len(stacks) + 2) + [IN_VMEM] * 4,
        out_specs=(IN_VMEM, IN_VMEM, *[ANYWHERE] * outs),
        scratch_shapes=[
            pltpu.VMEM((2, plan.channels, plan.channels), BF16),
            pltpu.VMEM((2, plan.span, plan.channels), BF16),
            pltpu.VMEM((count, plan.share, plan.channels), BF16),
            pltpu.VMEM((plan.span, plan.channels), BF16),
            pltpu.VMEM((plan.held, 8, plan.tok, plan.head), F32),
            pltpu.VMEM((plan.held, 2, plan.tok, plan.head), F32),
            pltpu.SemaphoreType.DMA((2, plan.ways)),
            pltpu.SemaphoreType.DMA((2,)),
            pltpu.SemaphoreType.DMA((1,)),
            pltpu.SemaphoreType.DMA((count,)),
        ],
        name="back",
        **params(6 * count * plan.span * plan.channels * plan.channels, 3 * count * plan.channels**2),
    )(scalars, *stacks, states, grad, cos, sin, gains, swap)


def first_back_kernel(scalars, *refs, plan):
    stacks, refs = refs[: plan.pieces], refs[plan.pieces :]
    rows, grad_any, cos_ref, sin_ref, gains, swap_ref, gain_out = refs[:7]
    buffer, hidden, grad_in, grad_mixed, tables, sums, sems, row_sems = refs[7:]
    base = scalars[plan.base_at]
    counts = [scalars[plan.counts_at + t].astype(F32) for t in range(plan.held)]
    copies = [
        pltpu.make_async_copy(grad_any, grad_in, row_sems.at[0]),
        pltpu.make_async_copy(rows.at[own_rows(plan, scalars)], hidden, row_sems.at[1]),
    ]
    start_all(copies)
    copies += load_weight(plan, scalars, stacks, 0, buffer, sems)
    fill_tables(tables, cos_ref, sin_ref, gains.at[scalars[plan.place_at]], swap_ref, base)
    wait_all(copies)
    pull_mixed(grad_in, buffer, grad_mixed, plan.width)
    gain_out[...] = pull_rows(
        hidden, grad_in, grad_mixed, tables, cos_ref, sin_ref, base, gains.at[scalars[plan.place_at]], swap_ref, counts, sums, None,
        plan.tok, plan.head, plan.heads,
    )


def first_back(plan, scalars, stacks, rows, grad_in, cos, sin, gains, swap):
    held = pltpu.VMEM((plan.span, plan.channels), BF16)
    return pl.pallas_call(
        functools.partial(first_back_kernel, plan=plan),
        out_shape=jax.ShapeDtypeStruct((GAIN_ROWS, plan.head), F32),
        in_specs=[IN_SMEM] + [ANYWHERE] * (len(stacks) + 2) + [IN_VMEM] * 4,
        out_specs=IN_VMEM,
        scratch_shapes=[
            pltpu.VMEM((plan.channels, plan.channels), BF16),
            held,
            held,
            held,
            pltpu.VMEM((plan.held, 8, plan.tok, plan.head), F32),
            pltpu.VMEM((plan.held, 2, plan.tok, plan.head), F32),
            pltpu.SemaphoreType.DMA((plan.ways,)),
            pltpu.SemaphoreType.DMA((2,)),
        ],
        name="first_back",
        **params(6 * plan.span * plan.channels * plan.channels, 3 * plan.channels**2),
    )(scalars, *stacks, rows, grad_in, cos, sin, gains, swap)


def turn_kernel(place, *refs, plan):
    rows, (out, gathered, turned, sems) = refs[: 2 * plan.depth], refs[2 * plan.depth :]
    copies = [
        pltpu.make_async_copy(source, gathered.at[pl.ds(at * plan.share, plan.share)], sems.at[at])
        for at, source in enumerate(rows)
    ]
    start_all(copies)
    wait_all(copies)

    def part(i, carry):
        cols = pl.ds(pl.multiple_of(i * plan.width, plan.width), plan.width)
        turned[cols, :] = gathered[:, cols].T
        return carry

    lax.fori_loop(0, plan.channels // plan.width, part, 0)
    for k in range(plan.chips):
        start = ((place[2] ^ k) * CORES + place[1]) * plan.rows
        out[k * plan.rows : (k + 1) * plan.rows, :] = turned[
            pl.ds(pl.multiple_of(start, math.gcd(plan.rows, 16)), plan.rows), :
        ]


def turn(plan, place, rows):
    total = 2 * plan.depth * plan.share
    return pl.pallas_call(
        functools.partial(turn_kernel, plan=plan),
        out_shape=jax.ShapeDtypeStruct((plan.chips * plan.rows, total), BF16),
        in_specs=[IN_SMEM] + [ANYWHERE] * len(rows),
        out_specs=IN_VMEM,
        scratch_shapes=[
            pltpu.VMEM((total, plan.channels), BF16),
            pltpu.VMEM((plan.channels, total), BF16),
            pltpu.SemaphoreType.DMA((2 * plan.depth,)),
        ],
        name="turn",
        **params(0, 4 * total * plan.channels),
    )(place, *rows)


def term_kernel(place, gain_ref, turned_any, cot, cot_other, *refs, plan, half):
    total = 2 * plan.depth
    rows, refs = refs[:total], refs[total:]
    outs, (turned, grads, terms, extra, sems, turned_sem, out_sems, extra_sems) = refs[: plan.chips], refs[plan.chips :]
    width = plan.channels // 2
    count = 1
    chunks = [pl.ds((count * half + i) * width, width) for i in range(count)]
    load = pltpu.make_async_copy(turned_any, turned, turned_sem.at[0])
    load.start()

    def gather(from_cotangent):
        for i, cols in enumerate(chunks):
            for at in range(total):
                side, k = divmod(at, plan.depth)
                if from_cotangent:
                    source = (cot, cot_other)[side].at[pl.ds((last ^ k) * plan.share, plan.share), cols]
                else:
                    source = rows[at].at[:, cols]
                target = grads.at[i, pl.ds(at * plan.share, plan.share)]
                pltpu.make_async_copy(source, target, sems.at[i, at]).start()

    last = plan.depth - 1
    pl.when(place[0] == last)(functools.partial(gather, True))
    pl.when(place[0] != last)(functools.partial(gather, False))
    going = []
    if half:
        extra[...] = jnp.zeros(extra.shape, BF16)
        left = gain_ref[...]
        for i in range(GAIN_PARTS):
            part = left.astype(BF16)
            extra[0:GAIN_ROWS, i * plan.head : (i + 1) * plan.head] = part
            left = left - part.astype(F32)
        for k in range(plan.chips):
            target = outs[k].at[pl.ds(plan.rows, EXTRA_ROWS)]
            going.append(pltpu.make_async_copy(extra, target, extra_sems.at[k]))
            going[-1].start()
    load.wait()
    for i, cols in enumerate(chunks):
        for at in range(total):
            piece = grads.at[i, pl.ds(at * plan.share, plan.share)]
            pltpu.make_async_copy(piece, piece, sems.at[i, at]).wait()
        terms[i] = jnp.dot(turned[...], grads[i], preferred_element_type=F32).astype(BF16)
        for k in range(plan.chips):
            target = outs[k].at[pl.ds(0, plan.rows), pl.ds(i * width, width)]
            source = terms.at[i, pl.ds(k * plan.rows, plan.rows)]
            going.append(pltpu.make_async_copy(source, target, out_sems.at[i, k]))
            going[-1].start()
    wait_all(going)


def term(plan, half, place, gain, turned, cot, cot_other, rows):
    total = 2 * plan.depth * plan.share
    width = plan.channels // 2
    count = 1
    return pl.pallas_call(
        functools.partial(term_kernel, plan=plan, half=half),
        out_shape=[jax.ShapeDtypeStruct((plan.rows + (EXTRA_ROWS if half else 0), plan.channels // 2), BF16)] * plan.chips,
        in_specs=[IN_SMEM, IN_VMEM] + [ANYWHERE] * (3 + len(rows)),
        out_specs=[ANYWHERE] * plan.chips,
        scratch_shapes=[
            pltpu.VMEM((plan.chips * plan.rows, total), BF16),
            pltpu.VMEM((count, total, width), BF16),
            pltpu.VMEM((count, plan.chips * plan.rows, width), BF16),
            pltpu.VMEM((EXTRA_ROWS, plan.channels // 2), BF16),
            pltpu.SemaphoreType.DMA((count, 2 * plan.depth)),
            pltpu.SemaphoreType.DMA((1,)),
            pltpu.SemaphoreType.DMA((count, plan.chips)),
            pltpu.SemaphoreType.DMA((plan.chips,)),
        ],
        name="term",
        **params(total * plan.channels**2, 4 * plan.channels**2),
    )(place, gain, turned, cot, cot_other, *rows)


def along_pipe(x, k):
    return lax.ppermute(x, "pipe", [(i, i ^ k) for i in range(lax.axis_size("pipe"))])


def along_chips(x, k):
    return lax.ppermute(x, "dp", [(i, i ^ (CORES * k)) for i in range(lax.axis_size("dp"))])


def other_core(x):
    return lax.ppermute(x, "dp", [(i, i ^ 1) for i in range(lax.axis_size("dp"))])


def spread_near(block, depth):
    return {1 << bit: along_pipe(block, 1 << bit) for bit in range(depth.bit_length() - 1)}


def spread_far(near, depth):
    bits = depth.bit_length() - 1
    part = near[1].shape[0] // bits
    got = {k: [x[i * part : (i + 1) * part] for i in range(bits)] for k, x in near.items()}
    for k in sorted(range(1, depth), key=lambda k: k.bit_count()):
        if k not in got:
            got[k] = []
            for i in range(bits):
                order = [(i + b) % bits for b in range(bits)]
                bit = 1 << [b for b in order if k >> b & 1][-1]
                got[k].append(along_pipe(got[k ^ bit][i], bit))
    return {k: parts for k, parts in got.items() if k not in near}


def gather_weights(plan, own, gain, chip, beside):
    chips, depth = plan.chips, plan.depth
    order = [sorted((b for b in range(chips) if b != c), key=lambda b: (abs(b - c), b ^ c)) for c in range(chips)]
    up = down = block = own
    arrived = {}
    ours, nears, theirs, gains, extra = [], [], [], (), ()

    def swapped(i, keys):
        return {k: [other_core(x) for x in ours[i][k]] for k in keys}

    near_keys = [k for k in range(depth) if k.bit_count() < 2]
    far_keys = [k for k in range(depth) if k.bit_count() > 1]

    for step in range(1, chips + 1):
        near = spread_near(block, depth)
        if step == 1:
            gains = [along_pipe(gain, k) for k in range(1, depth)]
        if step == 1:
            extra = beside(jnp.asarray([[c, *order[c]] for c in range(chips)], jnp.int32)[chip])
        far = spread_far(nears[-1], depth) if step > 1 else {}
        swaps = []
        if step > 2:
            swaps = [swapped(step - 3, range(depth))]
        if step < chips:
            up = lax.ppermute(up, "dp", [(i, i + CORES) for i in range(plan.ways - CORES)])
            down = lax.ppermute(down, "dp", [(i + CORES, i) for i in range(plan.ways - CORES)])
        up, down, near, gains, extra, swaps = lax.optimization_barrier(
            (up, down, near, gains, extra, swaps)
        )
        theirs += swaps
        if step > 1:
            ours[-1].update(far)
        nears.append(near)
        ours.append({0: [block], **{k: [x] for k, x in near.items()}})
        arrived[step, -1], arrived[step, 1] = up, down
        if step < chips:
            places = {}
            for c in range(chips):
                b = order[c][step - 1]
                places.setdefault((abs(b - c), 1 if b > c else -1), []).append(c)
            (first, _), *rest = places.items()
            block = arrived[first]
            for key, members in rest:
                here = functools.reduce(jnp.logical_or, [chip == c for c in members])
                block = jnp.where(here, arrived[key], block)
    far = spread_far(nears[-1], depth)
    left = [swapped(i, range(depth)) for i in range(len(theirs), chips - 1)] + [swapped(chips - 1, near_keys)]
    ours[-1].update(far)
    theirs += left
    theirs[-1].update(swapped(chips - 1, far_keys))
    pieces = [x for block in ours + theirs for k in range(depth) for x in block[k]]
    return pieces, jnp.stack([gain, *gains]).astype(F32), extra


def shards(clips, positions, out_proj, qk_gains, cotangent):
    plan = Plan(clips, out_proj, qk_gains)
    depth, last = plan.depth, plan.depth - 1
    place = lax.axis_index("pipe")
    member = lax.axis_index("dp")
    chip, core = member // CORES, member % CORES
    rows = clips.reshape(plan.tiles * plan.tok, plan.channels)
    last_grad = cotangent.reshape(plan.tiles * plan.tok, plan.channels)
    coord, freq, sign, partner = lane_tables(plan.head)
    own_gain = jnp.pad(qk_gains[0], ((0, GAIN_ROWS - 2), (0, 0)))
    first_row = place * plan.share
    base = jnp.minimum(first_row // plan.tok, plan.tiles - plan.held)
    tile_starts = (base + jnp.arange(plan.held)) * plan.tok
    counts = ((tile_starts >= first_row) & (tile_starts < first_row + plan.share)).astype(jnp.int32)

    def settings(whose):
        spots = positions.reshape(3, plan.tiles, plan.tok, 1).astype(F32)
        angle = jnp.where(coord == 0, spots[0], jnp.where(coord == 1, spots[1], spots[2])) * freq
        swap = jnp.asarray(np.eye(plan.head)[partner], BF16)
        starts = [(whose * CORES + core) * plan.rows, (whose * CORES + 1 - core) * plan.rows]
        more = jnp.stack([base, first_row - base * plan.tok, place])
        scalars = jnp.concatenate([*starts, more, counts]).astype(jnp.int32)
        return scalars, jnp.cos(angle), jnp.sin(angle) * sign, swap

    blocks, gains, (scalars, cos, sin, swap) = gather_weights(plan, out_proj[0], own_gain, chip, settings)
    setting = (cos, sin, gains, swap)

    def to_owners(windows, count):
        return [
            lax.ppermute(windows[k], "pipe", [(i, i ^ k) for i in range(depth) if i ^ k < count]) for k in range(1, depth)
        ]

    states, *mixed = forward(plan, scalars, blocks, rows, *setting)
    received = to_owners(mixed, depth)
    far = [k - 1 for k in range(1, depth) if k.bit_count() > 1]
    grad, terms, *windows = back(plan, range(last, 0, -1), scalars, blocks, states, last_grad, *setting)
    terms = terms[::-1]
    mixed_other, cot_other = other_core(mixed[0]), other_core(last_grad)
    grad, windows, received, mixed_other, cot_other = lax.optimization_barrier(
        (grad, windows, received, mixed_other, cot_other)
    )
    grads = to_owners(windows, last)
    first_term = first_back(plan, scalars, blocks, rows, grad, *setting)
    where = jnp.stack([place, core, chip]).astype(jnp.int32)
    windows_other = other_core(windows[0])
    turned = turn(plan, where, [mixed[0], *received, mixed_other, *[other_core(x) for x in received]])
    turned, windows_other, first_term, arrived = lax.optimization_barrier(
        (turned, windows_other, first_term, [grads[i] for i in far])
    )
    for i, x in zip(far, arrived):
        grads[i] = x

    grads_other = [other_core(x) for x in grads]
    given = (turned, last_grad, cot_other, [windows[0], *grads, windows_other, *grads_other])
    terms = jnp.concatenate([first_term[None], terms], axis=0)
    totals, gain_sum = [], first_term
    for half in range(2):
        if half:
            pieces[0], terms = lax.optimization_barrier((pieces[0], terms))
            gain_sum = lax.dynamic_index_in_dim(terms, place, 0, keepdims=False)
            for k in range(1, depth):
                sent = lax.dynamic_index_in_dim(terms, place ^ k, 0, keepdims=False)
                gain_sum = gain_sum + along_pipe(sent, k)
            gain_sum = gain_sum + other_core(gain_sum)
        pieces = list(term(plan, half, where, gain_sum, *given))
        parts = [pieces[0], *[along_chips(pieces[k], k) for k in range(1, plan.chips)]]
        totals.append(sum(part[: plan.rows].astype(F32) for part in parts))
    by_chip = jnp.stack([part[plan.rows : plan.rows + 2] for part in parts])[chip ^ jnp.arange(plan.chips)]
    gain_parts = jnp.sum(by_chip.astype(F32), axis=0)
    own_gains = sum(gain_parts[:, i * plan.head : (i + 1) * plan.head] for i in range(GAIN_PARTS))
    return (jnp.concatenate(totals, axis=1)[None], own_gains[None])


def solution(mesh):
    placed = (
        P(None, None, "dp", None),
        P(None, None, None, "dp"),
        P("pipe", "dp", None),
        P("pipe", None, None),
        P(None, None, "dp", None),
    )
    return jax.shard_map(
        shards,
        mesh=mesh,
        in_specs=placed,
        out_specs=(P("pipe", "dp", None), P("pipe", None, None)),
        check_vma=False,
    )
```

```python
import functools
import math

import jax
import jax.numpy as jnp
import numpy as np
from jax import lax
from jax.experimental import pallas as pl
from jax.experimental.pallas import tpu as pltpu
from jax.sharding import PartitionSpec as P

F32 = jnp.float32
BF16 = jnp.bfloat16
VMEM_BYTES = 56 * 1024 * 1024
CORES = 2
GAIN_ROWS = 8
GAIN_PARTS = 3
EXTRA_ROWS = 16


def lane_tables(head):
    first = head // 8
    rest = (head - first) // 2
    coord = np.zeros(head, np.int32)
    freq = np.zeros(head, np.float32)
    sign = np.zeros(head, np.float32)
    partner = np.zeros(head, np.int32)
    offset = 0
    for axis, width in enumerate((first, rest, rest)):
        half = width // 2
        for j in range(half):
            low, high = offset + j, offset + j + half
            coord[low] = coord[high] = axis
            freq[low] = freq[high] = 256.0 ** (-2.0 * j / width)
            sign[low], sign[high] = -1.0, 1.0
            partner[low], partner[high] = high, low
        offset += width
    return coord, freq, sign, partner


def nt(a, b):
    return lax.dot_general(a, b, (((1,), (1,)), ((), ())), preferred_element_type=F32)


def tn(a, b):
    return lax.dot_general(a, b, (((0,), (0,)), ((), ())), preferred_element_type=F32)


def split(x):
    high = x.astype(BF16)
    return high, (x - high.astype(F32)).astype(BF16)


def fill_tables(tables, cos_ref, sin_ref, gain_ref, swap_ref, first=0):
    gain = gain_ref[...]
    turned = jnp.dot(gain.astype(BF16), swap_ref[...], preferred_element_type=F32)
    factor = 1.0 / math.sqrt(gain.shape[-1])
    query, query_turned, key, key_turned = gain[0:1] * factor, turned[0:1] * factor, gain[1:2], turned[1:2]
    for t in range(tables.shape[0]):
        cosine, sine = cos_ref[first + t], sin_ref[first + t]
        tables[t, 0] = cosine * query
        tables[t, 1] = sine * query_turned
        tables[t, 2] = cosine * key
        tables[t, 3] = sine * key_turned
        if tables.shape[1] > 4:
            tables[t, 4] = cosine * query_turned
            tables[t, 5] = -sine * query
            tables[t, 6] = cosine * key_turned
            tables[t, 7] = -sine * key


def project(hidden, mixed, weight, out, width):
    def part(i, carry):
        cols = pl.ds(pl.multiple_of(i * width, width), width)
        update = jnp.dot(mixed[...], weight[:, cols], preferred_element_type=F32)
        out[:, cols] = (hidden[:, cols].astype(F32) + update).astype(BF16)
        return carry

    lax.fori_loop(0, out.shape[1] // width, part, 0)


def pull_mixed(grad, weight, grad_mixed, width):
    def part(i, carry):
        cols = pl.ds(pl.multiple_of(i * width, width), width)
        grad_mixed[:, cols] = nt(grad[...], weight[cols, :]).astype(BF16)
        return carry

    lax.fori_loop(0, grad_mixed.shape[1] // width, part, 0)


def head_stage(pairs, hidden, tables, swap):
    values = [hidden[r, c] for _, r, c in pairs]
    wide = [v.astype(F32) for v in values]
    scale = [lax.rsqrt(jnp.mean(x * x, axis=-1, keepdims=True) + 1e-06) for x in wide]
    turned = [jnp.dot(v, swap, preferred_element_type=F32) * s for v, s in zip(values, scale)]
    normed = [x * s for x, s in zip(wide, scale)]
    queries = [split(n * tables[t, 0] + w * tables[t, 1]) for (t, _, _), n, w in zip(pairs, normed, turned)]
    keys = [split(n * tables[t, 2] + w * tables[t, 3]) for (t, _, _), n, w in zip(pairs, normed, turned)]
    scores = [
        nt(jnp.concatenate([qh, ql, qh], axis=1), jnp.concatenate([kh, kh, kl], axis=1))
        for (qh, ql), (kh, kl) in zip(queries, keys)
    ]
    raised = [jnp.exp(s) for s in scores]
    weights = [e * (1.0 / jnp.sum(e, axis=-1, keepdims=True)) for e in raised]
    return values, normed, turned, scale, [q[0] for q in queries], [k[0] for k in keys], weights


def head_pairs(step, groups, tok, head, together):
    cols = [pl.ds(pl.multiple_of((step * together + u) * head, head), head) for u in range(together)]
    return [(t, slice(t * tok, (t + 1) * tok), c) for c in cols for t in range(groups)]


def mix_rows(hidden, tables, swap_ref, mixed, tok, head, together):
    groups = hidden.shape[0] // tok
    swap = swap_ref[...]

    def some(i, carry):
        pairs = head_pairs(i, groups, tok, head, together)
        values, _, _, _, _, _, weights = head_stage(pairs, hidden, tables, swap)
        rounded = [w.astype(BF16) for w in weights]
        results = [jnp.dot(w, v, preferred_element_type=F32).astype(BF16) for w, v in zip(rounded, values)]
        for (_, r, c), m in zip(pairs, results):
            mixed[r, c] = m
        return carry

    lax.fori_loop(0, hidden.shape[1] // head // together, some, 0)


def pull_rows(
    hidden, grad, grad_mixed, tables, cos_ref, sin_ref, first, gain_ref, swap_ref, counts, sums, out, tok, head, together
):
    groups = hidden.shape[0] // tok
    swap = swap_ref[...]
    factor = 1.0 / math.sqrt(head)
    gain_q, gain_k = gain_ref[0:1, :] * factor, gain_ref[1:2, :]
    sums[...] = jnp.zeros(sums.shape, F32)

    def some(i, carry):
        pairs = head_pairs(i, groups, tok, head, together)
        values, normed, turned, scale, queries, keys, weights = head_stage(pairs, hidden, tables, swap)
        queries = [
            jnp.concatenate([q, (w * tables[t, 4] + n * tables[t, 5]).astype(BF16)], axis=1)
            for (t, _, _), q, n, w in zip(pairs, queries, normed, turned)
        ]
        keys = [
            jnp.concatenate([k, (w * tables[t, 6] + n * tables[t, 7]).astype(BF16)], axis=1)
            for (t, _, _), k, n, w in zip(pairs, keys, normed, turned)
        ]
        above = [grad_mixed[r, c] for _, r, c in pairs]
        grad_weights = [nt(a, v).astype(BF16).astype(F32) for a, v in zip(above, values)]
        if out is not None:
            grad_values = [tn(w.astype(BF16), a) for w, a in zip(weights, above)]
        means = [jnp.sum(g * w, axis=-1, keepdims=True) for g, w in zip(grad_weights, weights)]
        grad_scores = [(w * (g - m)).astype(BF16) for w, g, m in zip(weights, grad_weights, means)]
        grad_q = [jnp.dot(s, k, preferred_element_type=F32) for s, k in zip(grad_scores, keys)]
        grad_k = [tn(s, q) for s, q in zip(grad_scores, queries)]
        back_q = [g[:, :head] * cos_ref[first + p[0]] - g[:, head:] * sin_ref[first + p[0]] for p, g in zip(pairs, grad_q)]
        back_k = [g[:, :head] * cos_ref[first + p[0]] - g[:, head:] * sin_ref[first + p[0]] for p, g in zip(pairs, grad_k)]
        for t in range(groups):
            mine = [j for j, p in enumerate(pairs) if p[0] == t]
            sums[t, 0] += sum(normed[j] * back_q[j] for j in mine)
            sums[t, 1] += sum(normed[j] * back_k[j] for j in mine)
        if out is not None:
            grad_normed = [q * gain_q + k * gain_k for q, k in zip(back_q, back_k)]
            along = [jnp.mean(n * g, axis=-1, keepdims=True) for n, g in zip(normed, grad_normed)]
            grad_hidden = [
                (v + s * (g - n * a)).astype(BF16).astype(F32)
                for v, s, g, n, a in zip(grad_values, scale, grad_normed, normed, along)
            ]
            for (_, r, c), g in zip(pairs, grad_hidden):
                out[r, c] = (grad[r, c].astype(F32) + g).astype(BF16)
        return carry

    lax.fori_loop(0, hidden.shape[1] // head // together, some, 0)
    total = [
        sum(counts[t] * jnp.sum(sums[t, i], axis=0, keepdims=True) for t in range(groups)) for i in range(2)
    ]
    return jnp.concatenate([total[0] * factor, total[1], jnp.zeros((GAIN_ROWS - 2, head), F32)], axis=0)


def params(flops, size):
    return dict(
        compiler_params=pltpu.CompilerParams(vmem_limit_bytes=VMEM_BYTES),
        cost_estimate=pl.CostEstimate(flops=flops, bytes_accessed=size, transcendentals=0),
    )


IN_VMEM = pl.BlockSpec(memory_space=pltpu.VMEM)
IN_SMEM = pl.BlockSpec(memory_space=pltpu.SMEM)
ANYWHERE = pl.BlockSpec(memory_space=pl.ANY)


class Plan:
    def parts_of(self, k):
        return 1 if k.bit_count() < 2 else self.depth.bit_length() - 1

    def __init__(self, clips, out_proj, qk_gains):
        self.depth = lax.axis_size("pipe")
        self.ways = lax.axis_size("dp")
        self.tok = clips.shape[2]
        self.channels = clips.shape[3]
        self.head = qk_gains.shape[-1]
        self.heads = self.channels // self.head
        self.tiles = clips.shape[0] * clips.shape[1]
        self.rows = out_proj.shape[1]
        self.share = self.tiles * self.tok // self.depth
        self.held = max(-(-(p * self.share % self.tok + self.share) // self.tok) for p in range(self.depth))
        self.span = self.held * self.tok
        self.width = math.gcd(self.channels, 768)
        self.chips = self.ways // CORES
        self.base_at = self.ways
        self.pieces = self.ways * sum(self.parts_of(k) for k in range(self.depth))
        self.window_at = self.base_at + 1
        self.place_at = self.base_at + 2
        self.counts_at = self.base_at + 3


def load_weight(plan, scalars, pieces, phase, buffer, sems):
    waits = []
    refs = iter(pieces)
    for i in range(plan.ways):
        first = scalars[i]
        for k in range(plan.depth):
            parts = plan.parts_of(k)
            size = plan.rows // parts
            copies = []
            for j in range(parts):
                rows = pl.ds(pl.multiple_of(first + j * size, math.gcd(size, 16)), size)
                copies.append(pltpu.make_async_copy(next(refs), buffer.at[rows], sems.at[i]))
            pl.when(scalars[plan.place_at] == phase ^ k)(functools.partial(start_all, copies))
        rows = buffer.at[pl.ds(pl.multiple_of(first, math.gcd(plan.rows, 16)), plan.rows)]
        waits.append(pltpu.make_async_copy(rows, rows, sems.at[i]))
    return waits


def start_all(copies):
    for copy in copies:
        copy.start()


def wait_all(copies):
    for copy in copies:
        copy.wait()


def window_of(plan, scalars):
    return pl.ds(pl.multiple_of(scalars[plan.window_at], math.gcd(plan.share, plan.tok)), plan.share)


def own_rows(plan, scalars):
    return pl.ds(pl.multiple_of(scalars[plan.base_at] * plan.tok, plan.tok), plan.span)


def to_owner(plan, scalars, phase, rows, outs, sem):
    for k, out in enumerate(outs):
        copy = pltpu.make_async_copy(rows, out, sem)
        pl.when(scalars[plan.place_at] == phase ^ k)(copy.start)
    return copy


def forward_kernel(scalars, *refs, plan):
    stacks, refs = refs[: plan.pieces], refs[plan.pieces :]
    rows, cos_ref, sin_ref, gains, swap_ref = refs[:5]
    states_out, sent_out, refs = refs[5], refs[6 : 6 + plan.depth], refs[6 + plan.depth :]
    buffer, start, states, sent, mixed, tables, sems, row_sem, state_sems, sent_sems = refs
    last = plan.depth - 1
    base = scalars[plan.base_at]
    load = pltpu.make_async_copy(rows.at[own_rows(plan, scalars)], start, row_sem.at[0])
    load.start()

    def fetch(phase):
        return load_weight(plan, scalars, stacks, phase, buffer.at[phase % 2], sems.at[phase % 2])

    coming = {phase: fetch(phase) for phase in range(min(2, last))}
    going = []
    for phase in range(plan.depth):
        hidden = states.at[phase - 1] if phase else start
        fill_tables(tables, cos_ref, sin_ref, gains.at[scalars[plan.place_at] ^ phase], swap_ref, base)
        if phase == 0:
            load.wait()
        mix_rows(hidden, tables, swap_ref, mixed, plan.tok, plan.head, plan.heads)
        sent[phase] = mixed[window_of(plan, scalars), :]
        going.append(to_owner(plan, scalars, phase, sent.at[phase], sent_out, sent_sems.at[phase]))
        if phase < last:
            wait_all(coming[phase])
            project(hidden, mixed, buffer.at[phase % 2], states.at[phase], plan.width)
            going.append(pltpu.make_async_copy(states.at[phase], states_out.at[phase], state_sems.at[phase]))
            going[-1].start()
            if phase + 2 < last:
                coming[phase + 2] = fetch(phase + 2)
    wait_all(going)


def forward(plan, scalars, stacks, rows, cos, sin, gains, swap):
    shape = jax.ShapeDtypeStruct
    states = (plan.depth - 1, plan.span, plan.channels)
    return pl.pallas_call(
        functools.partial(forward_kernel, plan=plan),
        out_shape=(shape(states, BF16), *[shape((plan.share, plan.channels), BF16)] * plan.depth),
        in_specs=[IN_SMEM] + [ANYWHERE] * (len(stacks) + 1) + [IN_VMEM] * 4,
        out_specs=(ANYWHERE,) * (plan.depth + 1),
        scratch_shapes=[
            pltpu.VMEM((2, plan.channels, plan.channels), BF16),
            pltpu.VMEM((plan.span, plan.channels), BF16),
            pltpu.VMEM(states, BF16),
            pltpu.VMEM((plan.depth, plan.share, plan.channels), BF16),
            pltpu.VMEM((plan.span, plan.channels), BF16),
            pltpu.VMEM((plan.held, 4, plan.tok, plan.head), F32),
            pltpu.SemaphoreType.DMA((2, plan.ways)),
            pltpu.SemaphoreType.DMA((1,)),
            pltpu.SemaphoreType.DMA((plan.depth - 1,)),
            pltpu.SemaphoreType.DMA((plan.depth,)),
        ],
        name="forward",
        **params(2 * plan.depth * plan.span * plan.channels * plan.channels, 2 * plan.depth * plan.channels**2),
    )(scalars, *stacks, rows, cos, sin, gains, swap)


def back_kernel(scalars, *refs, plan, phases):
    stacks, refs = refs[: plan.pieces], refs[plan.pieces :]
    states, grad_any, cos_ref, sin_ref, gains, swap_ref = refs[:6]
    top, count = phases[0], len(phases)
    outs = plan.depth
    grad_out, gain_out, sent_out, refs = refs[6], refs[7], refs[8 : 8 + outs], refs[8 + outs :]
    buffer, hidden, sent, grad_mixed, tables, sums, sems, state_sems, row_sem, sent_sems = refs
    base = scalars[plan.base_at]
    counts = [scalars[plan.counts_at + t].astype(F32) for t in range(plan.held)]
    source = grad_any.at[own_rows(plan, scalars)] if top == plan.depth - 1 else grad_any
    load = pltpu.make_async_copy(source, grad_out, row_sem.at[0])
    load.start()

    def fetch(phase):
        slot = phase % 2
        waits = load_weight(plan, scalars, stacks, phase, buffer.at[slot], sems.at[slot])
        waits.append(pltpu.make_async_copy(states.at[phase - 1], hidden.at[slot], state_sems.at[slot]))
        waits[-1].start()
        return waits

    coming = {phase: fetch(phase) for phase in phases[:2]}
    load.wait()
    going = []
    for i, phase in enumerate(phases):
        slot = phase % 2
        fill_tables(tables, cos_ref, sin_ref, gains.at[scalars[plan.place_at] ^ phase], swap_ref, base)
        wait_all(coming[phase])
        pull_mixed(grad_out, buffer.at[slot], grad_mixed, plan.width)
        gain_out[i] = pull_rows(
            hidden.at[slot], grad_out, grad_mixed, tables, cos_ref, sin_ref, base, gains.at[scalars[plan.place_at] ^ phase], swap_ref, counts,
            sums, grad_out, plan.tok, plan.head, plan.heads,
        )
        sent[i] = grad_out[window_of(plan, scalars), :]
        going.append(to_owner(plan, scalars, phase - 1, sent.at[i], sent_out, sent_sems.at[i]))
        if phase - 2 in phases:
            coming[phase - 2] = fetch(phase - 2)
    wait_all(going)


def back(plan, phases, scalars, stacks, states, grad, cos, sin, gains, swap):
    shape = jax.ShapeDtypeStruct
    count = len(phases)
    outs = plan.depth
    return pl.pallas_call(
        functools.partial(back_kernel, plan=plan, phases=phases),
        out_shape=(
            shape((plan.span, plan.channels), BF16),
            shape((count, GAIN_ROWS, plan.head), F32),
            *[shape((plan.share, plan.channels), BF16)] * outs,
        ),
        in_specs=[IN_SMEM] + [ANYWHERE] * (len(stacks) + 2) + [IN_VMEM] * 4,
        out_specs=(IN_VMEM, IN_VMEM, *[ANYWHERE] * outs),
        scratch_shapes=[
            pltpu.VMEM((2, plan.channels, plan.channels), BF16),
            pltpu.VMEM((2, plan.span, plan.channels), BF16),
            pltpu.VMEM((count, plan.share, plan.channels), BF16),
            pltpu.VMEM((plan.span, plan.channels), BF16),
            pltpu.VMEM((plan.held, 8, plan.tok, plan.head), F32),
            pltpu.VMEM((plan.held, 2, plan.tok, plan.head), F32),
            pltpu.SemaphoreType.DMA((2, plan.ways)),
            pltpu.SemaphoreType.DMA((2,)),
            pltpu.SemaphoreType.DMA((1,)),
            pltpu.SemaphoreType.DMA((count,)),
        ],
        name="back",
        **params(6 * count * plan.span * plan.channels * plan.channels, 3 * count * plan.channels**2),
    )(scalars, *stacks, states, grad, cos, sin, gains, swap)


def first_back_kernel(scalars, *refs, plan):
    stacks, refs = refs[: plan.pieces], refs[plan.pieces :]
    rows, grad_any, cos_ref, sin_ref, gains, swap_ref, gain_out = refs[:7]
    buffer, hidden, grad_in, grad_mixed, tables, sums, sems, row_sems = refs[7:]
    base = scalars[plan.base_at]
    counts = [scalars[plan.counts_at + t].astype(F32) for t in range(plan.held)]
    copies = [
        pltpu.make_async_copy(grad_any, grad_in, row_sems.at[0]),
        pltpu.make_async_copy(rows.at[own_rows(plan, scalars)], hidden, row_sems.at[1]),
    ]
    start_all(copies)
    copies += load_weight(plan, scalars, stacks, 0, buffer, sems)
    fill_tables(tables, cos_ref, sin_ref, gains.at[scalars[plan.place_at]], swap_ref, base)
    wait_all(copies)
    pull_mixed(grad_in, buffer, grad_mixed, plan.width)
    gain_out[...] = pull_rows(
        hidden, grad_in, grad_mixed, tables, cos_ref, sin_ref, base, gains.at[scalars[plan.place_at]], swap_ref, counts, sums, None,
        plan.tok, plan.head, plan.heads,
    )


def first_back(plan, scalars, stacks, rows, grad_in, cos, sin, gains, swap):
    held = pltpu.VMEM((plan.span, plan.channels), BF16)
    return pl.pallas_call(
        functools.partial(first_back_kernel, plan=plan),
        out_shape=jax.ShapeDtypeStruct((GAIN_ROWS, plan.head), F32),
        in_specs=[IN_SMEM] + [ANYWHERE] * (len(stacks) + 2) + [IN_VMEM] * 4,
        out_specs=IN_VMEM,
        scratch_shapes=[
            pltpu.VMEM((plan.channels, plan.channels), BF16),
            held,
            held,
            held,
            pltpu.VMEM((plan.held, 8, plan.tok, plan.head), F32),
            pltpu.VMEM((plan.held, 2, plan.tok, plan.head), F32),
            pltpu.SemaphoreType.DMA((plan.ways,)),
            pltpu.SemaphoreType.DMA((2,)),
        ],
        name="first_back",
        **params(6 * plan.span * plan.channels * plan.channels, 3 * plan.channels**2),
    )(scalars, *stacks, rows, grad_in, cos, sin, gains, swap)


def turn_kernel(place, *refs, plan):
    rows, (out, gathered, turned, sems) = refs[: 2 * plan.depth], refs[2 * plan.depth :]
    copies = [
        pltpu.make_async_copy(source, gathered.at[pl.ds(at * plan.share, plan.share)], sems.at[at])
        for at, source in enumerate(rows)
    ]
    start_all(copies)
    wait_all(copies)

    def part(i, carry):
        cols = pl.ds(pl.multiple_of(i * plan.width, plan.width), plan.width)
        turned[cols, :] = gathered[:, cols].T
        return carry

    lax.fori_loop(0, plan.channels // plan.width, part, 0)
    for k in range(plan.chips):
        start = ((place[2] ^ k) * CORES + place[1]) * plan.rows
        out[k * plan.rows : (k + 1) * plan.rows, :] = turned[
            pl.ds(pl.multiple_of(start, math.gcd(plan.rows, 16)), plan.rows), :
        ]


def turn(plan, place, rows):
    total = 2 * plan.depth * plan.share
    return pl.pallas_call(
        functools.partial(turn_kernel, plan=plan),
        out_shape=jax.ShapeDtypeStruct((plan.chips * plan.rows, total), BF16),
        in_specs=[IN_SMEM] + [ANYWHERE] * len(rows),
        out_specs=IN_VMEM,
        scratch_shapes=[
            pltpu.VMEM((total, plan.channels), BF16),
            pltpu.VMEM((plan.channels, total), BF16),
            pltpu.SemaphoreType.DMA((2 * plan.depth,)),
        ],
        name="turn",
        **params(0, 4 * total * plan.channels),
    )(place, *rows)


def term_kernel(place, gain_ref, turned_any, cot, cot_other, *refs, plan, half):
    total = 2 * plan.depth
    rows, refs = refs[:total], refs[total:]
    outs, (turned, grads, terms, extra, sems, turned_sem, out_sems, extra_sems) = refs[: plan.chips], refs[plan.chips :]
    width = plan.channels // 2
    count = 1
    chunks = [pl.ds((count * half + i) * width, width) for i in range(count)]
    load = pltpu.make_async_copy(turned_any, turned, turned_sem.at[0])
    load.start()

    def gather(from_cotangent):
        for i, cols in enumerate(chunks):
            for at in range(total):
                side, k = divmod(at, plan.depth)
                if from_cotangent:
                    source = (cot, cot_other)[side].at[pl.ds((last ^ k) * plan.share, plan.share), cols]
                else:
                    source = rows[at].at[:, cols]
                target = grads.at[i, pl.ds(at * plan.share, plan.share)]
                pltpu.make_async_copy(source, target, sems.at[i, at]).start()

    last = plan.depth - 1
    pl.when(place[0] == last)(functools.partial(gather, True))
    pl.when(place[0] != last)(functools.partial(gather, False))
    going = []
    if half:
        extra[...] = jnp.zeros(extra.shape, BF16)
        left = gain_ref[...]
        for i in range(GAIN_PARTS):
            part = left.astype(BF16)
            extra[0:GAIN_ROWS, i * plan.head : (i + 1) * plan.head] = part
            left = left - part.astype(F32)
        for k in range(plan.chips):
            target = outs[k].at[pl.ds(plan.rows, EXTRA_ROWS)]
            going.append(pltpu.make_async_copy(extra, target, extra_sems.at[k]))
            going[-1].start()
    load.wait()
    for i, cols in enumerate(chunks):
        for at in range(total):
            piece = grads.at[i, pl.ds(at * plan.share, plan.share)]
            pltpu.make_async_copy(piece, piece, sems.at[i, at]).wait()
        terms[i] = jnp.dot(turned[...], grads[i], preferred_element_type=F32).astype(BF16)
        for k in range(plan.chips):
            target = outs[k].at[pl.ds(0, plan.rows), pl.ds(i * width, width)]
            source = terms.at[i, pl.ds(k * plan.rows, plan.rows)]
            going.append(pltpu.make_async_copy(source, target, out_sems.at[i, k]))
            going[-1].start()
    wait_all(going)


def term(plan, half, place, gain, turned, cot, cot_other, rows):
    total = 2 * plan.depth * plan.share
    width = plan.channels // 2
    count = 1
    return pl.pallas_call(
        functools.partial(term_kernel, plan=plan, half=half),
        out_shape=[jax.ShapeDtypeStruct((plan.rows + (EXTRA_ROWS if half else 0), plan.channels // 2), BF16)] * plan.chips,
        in_specs=[IN_SMEM, IN_VMEM] + [ANYWHERE] * (3 + len(rows)),
        out_specs=[ANYWHERE] * plan.chips,
        scratch_shapes=[
            pltpu.VMEM((plan.chips * plan.rows, total), BF16),
            pltpu.VMEM((count, total, width), BF16),
            pltpu.VMEM((count, plan.chips * plan.rows, width), BF16),
            pltpu.VMEM((EXTRA_ROWS, plan.channels // 2), BF16),
            pltpu.SemaphoreType.DMA((count, 2 * plan.depth)),
            pltpu.SemaphoreType.DMA((1,)),
            pltpu.SemaphoreType.DMA((count, plan.chips)),
            pltpu.SemaphoreType.DMA((plan.chips,)),
        ],
        name="term",
        **params(total * plan.channels**2, 4 * plan.channels**2),
    )(place, gain, turned, cot, cot_other, *rows)


def along_pipe(x, k):
    return lax.ppermute(x, "pipe", [(i, i ^ k) for i in range(lax.axis_size("pipe"))])


def along_chips(x, k):
    return lax.ppermute(x, "dp", [(i, i ^ (CORES * k)) for i in range(lax.axis_size("dp"))])


def other_core(x):
    return lax.ppermute(x, "dp", [(i, i ^ 1) for i in range(lax.axis_size("dp"))])


def spread_near(block, depth):
    return {1 << bit: along_pipe(block, 1 << bit) for bit in range(depth.bit_length() - 1)}


def spread_far(near, depth):
    bits = depth.bit_length() - 1
    part = near[1].shape[0] // bits
    got = {k: [x[i * part : (i + 1) * part] for i in range(bits)] for k, x in near.items()}
    for k in sorted(range(1, depth), key=lambda k: k.bit_count()):
        if k not in got:
            got[k] = []
            for i in range(bits):
                order = [(i + b) % bits for b in range(bits)]
                bit = 1 << [b for b in order if k >> b & 1][-1]
                got[k].append(along_pipe(got[k ^ bit][i], bit))
    return {k: parts for k, parts in got.items() if k not in near}


def gather_weights(plan, own, gain, chip, beside):
    chips, depth = plan.chips, plan.depth
    order = [sorted((b for b in range(chips) if b != c), key=lambda b: (abs(b - c), b ^ c)) for c in range(chips)]
    up = down = block = own
    arrived = {}
    ours, nears, theirs, gains, extra = [], [], [], (), ()

    def swapped(i, keys):
        return {k: [other_core(x) for x in ours[i][k]] for k in keys}

    near_keys = [k for k in range(depth) if k.bit_count() < 2]
    far_keys = [k for k in range(depth) if k.bit_count() > 1]

    for step in range(1, chips + 1):
        near = spread_near(block, depth)
        if step == 1:
            gains = [along_pipe(gain, k) for k in range(1, depth)]
        if step == 1:
            extra = beside(jnp.asarray([[c, *order[c]] for c in range(chips)], jnp.int32)[chip])
        far = spread_far(nears[-1], depth) if step > 1 else {}
        swaps = []
        if step > 2:
            swaps = [swapped(step - 3, range(depth))]
        if step < chips:
            up = lax.ppermute(up, "dp", [(i, i + CORES) for i in range(plan.ways - CORES)])
            down = lax.ppermute(down, "dp", [(i + CORES, i) for i in range(plan.ways - CORES)])
        up, down, near, gains, extra, swaps = lax.optimization_barrier(
            (up, down, near, gains, extra, swaps)
        )
        theirs += swaps
        if step > 1:
            ours[-1].update(far)
        nears.append(near)
        ours.append({0: [block], **{k: [x] for k, x in near.items()}})
        arrived[step, -1], arrived[step, 1] = up, down
        if step < chips:
            places = {}
            for c in range(chips):
                b = order[c][step - 1]
                places.setdefault((abs(b - c), 1 if b > c else -1), []).append(c)
            (first, _), *rest = places.items()
            block = arrived[first]
            for key, members in rest:
                here = functools.reduce(jnp.logical_or, [chip == c for c in members])
                block = jnp.where(here, arrived[key], block)
    far = spread_far(nears[-1], depth)
    left = [swapped(i, range(depth)) for i in range(len(theirs), chips - 1)] + [swapped(chips - 1, near_keys)]
    ours[-1].update(far)
    theirs += left
    theirs[-1].update(swapped(chips - 1, far_keys))
    pieces = [x for block in ours + theirs for k in range(depth) for x in block[k]]
    return pieces, jnp.stack([gain, *gains]).astype(F32), extra


def shards(clips, positions, out_proj, qk_gains, cotangent):
    plan = Plan(clips, out_proj, qk_gains)
    depth, last = plan.depth, plan.depth - 1
    place = lax.axis_index("pipe")
    member = lax.axis_index("dp")
    chip, core = member // CORES, member % CORES
    rows = clips.reshape(plan.tiles * plan.tok, plan.channels)
    last_grad = cotangent.reshape(plan.tiles * plan.tok, plan.channels)
    coord, freq, sign, partner = lane_tables(plan.head)
    own_gain = jnp.pad(qk_gains[0], ((0, GAIN_ROWS - 2), (0, 0)))
    first_row = place * plan.share
    base = jnp.minimum(first_row // plan.tok, plan.tiles - plan.held)
    tile_starts = (base + jnp.arange(plan.held)) * plan.tok
    counts = ((tile_starts >= first_row) & (tile_starts < first_row + plan.share)).astype(jnp.int32)

    def settings(whose):
        spots = positions.reshape(3, plan.tiles, plan.tok, 1).astype(F32)
        angle = jnp.where(coord == 0, spots[0], jnp.where(coord == 1, spots[1], spots[2])) * freq
        swap = jnp.asarray(np.eye(plan.head)[partner], BF16)
        starts = [(whose * CORES + core) * plan.rows, (whose * CORES + 1 - core) * plan.rows]
        more = jnp.stack([base, first_row - base * plan.tok, place])
        scalars = jnp.concatenate([*starts, more, counts]).astype(jnp.int32)
        return scalars, jnp.cos(angle), jnp.sin(angle) * sign, swap

    blocks, gains, (scalars, cos, sin, swap) = gather_weights(plan, out_proj[0], own_gain, chip, settings)
    setting = (cos, sin, gains, swap)

    def to_owners(windows, count):
        return [
            lax.ppermute(windows[k], "pipe", [(i, i ^ k) for i in range(depth) if i ^ k < count]) for k in range(1, depth)
        ]

    states, *mixed = forward(plan, scalars, blocks, rows, *setting)
    received = to_owners(mixed, depth)
    far = [k - 1 for k in range(1, depth) if k.bit_count() > 1]
    grad, terms, *windows = back(plan, range(last, 0, -1), scalars, blocks, states, last_grad, *setting)
    terms = terms[::-1]
    mixed_other, cot_other = other_core(mixed[0]), other_core(last_grad)
    grad, windows, received, mixed_other, cot_other = lax.optimization_barrier(
        (grad, windows, received, mixed_other, cot_other)
    )
    grads = to_owners(windows, last)
    first_term = first_back(plan, scalars, blocks, rows, grad, *setting)
    where = jnp.stack([place, core, chip]).astype(jnp.int32)
    windows_other = other_core(windows[0])
    turned = turn(plan, where, [mixed[0], *received, mixed_other, *[other_core(x) for x in received]])
    turned, windows_other, first_term, arrived = lax.optimization_barrier(
        (turned, windows_other, first_term, [grads[i] for i in far])
    )
    for i, x in zip(far, arrived):
        grads[i] = x

    grads_other = [other_core(x) for x in grads]
    given = (turned, last_grad, cot_other, [windows[0], *grads, windows_other, *grads_other])
    terms = jnp.concatenate([first_term[None], terms], axis=0)
    totals, gain_sum = [], first_term
    for half in range(2):
        if half:
            pieces[0], terms = lax.optimization_barrier((pieces[0], terms))
            gain_sum = lax.dynamic_index_in_dim(terms, place, 0, keepdims=False)
            for k in range(1, depth):
                sent = lax.dynamic_index_in_dim(terms, place ^ k, 0, keepdims=False)
                gain_sum = gain_sum + along_pipe(sent, k)
            gain_sum = gain_sum + other_core(gain_sum)
        pieces = list(term(plan, half, where, gain_sum, *given))
        parts = [pieces[0], *[along_chips(pieces[k], k) for k in range(1, plan.chips)]]
        totals.append(sum(part[: plan.rows].astype(F32) for part in parts))
    by_chip = jnp.stack([part[plan.rows : plan.rows + 2] for part in parts])[chip ^ jnp.arange(plan.chips)]
    gain_parts = jnp.sum(by_chip.astype(F32), axis=0)
    own_gains = sum(gain_parts[:, i * plan.head : (i + 1) * plan.head] for i in range(GAIN_PARTS))
    return (jnp.concatenate(totals, axis=1)[None], own_gains[None])


def solution(mesh):
    placed = (
        P(None, None, "dp", None),
        P(None, None, None, "dp"),
        P("pipe", "dp", None),
        P("pipe", None, None),
        P(None, None, "dp", None),
    )
    return jax.shard_map(
        shards,
        mesh=mesh,
        in_specs=placed,
        out_specs=(P("pipe", "dp", None), P("pipe", None, None)),
        check_vma=False,
    )
```
